512 devices in a mesh: lev: 2 (over core), lat: 8 (over z_lo, x), lon: 32 (over z_hi, y).
Axes of the slice: x: 4, y: 8, z: 8 (z_hi: 4, z_lo: 2; z = z_hi * 2 + z_lo), core: 2. Of those that a mesh axis runs over, the one named last changes fastest.
Arguments:
- tokens: bfloat16 [4, 48, 768, 384], P('lev', 'lat', 'lon'), may hold values from -6 to 6
- cotangent: bfloat16 [4, 48, 768, 384], P('lev', 'lat', 'lon'), may hold values from -6 to 6
- w_qkv: bfloat16 [384, 1152], replicated, may hold values from -16 to 16, as said below
- w_proj: bfloat16 [384, 384], replicated, may hold values from -0.609375 to 0.609375
- bias_table: float32 [8, 12, 3312], P('lat'), may hold values from -5 to 5
- bias_index: int32 [8, 144, 144], P('lat'), may hold values from 0 to 3311
- region_ids: int32 [48, 768], P('lat', 'lon'), may hold values from 0 to 2
Outputs:
- block_out: bfloat16 [4, 48, 768, 384], P('lev', 'lat', 'lon')
- grad_tokens: bfloat16 [4, 48, 768, 384], P('lev', 'lat', 'lon')
- grad_qkv: float32 [384, 1152], P('lat', ('lev', 'lon'))
- grad_proj: float32 [384, 384], P('lat', ('lev', 'lon'))
- grad_table: float32 [8, 12, 3312], P('lat')
The draws below stay inside these ranges and needn't reach their ends.
Inputs may be any that keep to these rules, and one draw needn't show every extreme that they name: `w_qkv`: columns 0 to 383 project queries, 384 to 767 keys, the rest values.
All inputs are finite; a program needn't handle non-finite values.
Results may differ from the reference program's by a relative error of at most 0.012.
The reference program's roundings to bfloat16 on the way count: a program that leaves them out, or rounds other values in their place, can miss the bound.
Values may be sent and summed in bfloat16 or wider, within the bound.
A program may use at most 64 MiB of HBM per device.

```python
import jax
import jax.numpy as jnp
from jax import lax

C = 384
HEADS = 12
WLEV = 2
WLAT = 6
WLON = 12
WIN = 144
POS = 3312
LEVELS = 4
NLAT = 48
NLON = 768
TYPES = 8
TOKENS = 147456


def draw_w_qkv(key, part):
    key = jax.random.fold_in(key, 11)
    base = jax.random.truncated_normal(key, -6.0, 6.0, (C, 3 * C), jnp.float32) * C ** (-0.5)
    return base.astype(jnp.bfloat16)


def plant(result, stream_key, least, high):
    place = [jax.random.randint(jax.random.fold_in(stream_key, axis), (), 0, length) for axis, length in enumerate(result.shape)]
    longest = result.shape.index(max(result.shape))
    neighbour = place[:longest] + [(place[longest] + 1) % result.shape[longest]] + place[longest + 1:]
    return result.at[tuple(place)].set(least).at[tuple(neighbour)].set(high)


def block_scale(stream_key, shape, pieces, smallest, high):
    def one(axis_at, parts):
        heights = jax.random.uniform(jax.random.fold_in(jax.random.fold_in(stream_key, 6), axis_at), (parts,), jnp.float32, smallest / len(pieces), high / len(pieces))
        return jnp.repeat(jnp.exp(heights), shape[axis_at] // parts).reshape((-1,) + (1,) * (len(shape) - axis_at - 1))

    loudness = one(*pieces[0])
    for cut in pieces[1:]:
        loudness = loudness * one(*cut)
    return loudness


def bell_draw(rng, extent, scale, limit, pieces=(), dtype=jnp.bfloat16):
    factor_of = block_scale(rng, extent, pieces, -0.22, 0.18) if pieces else 1.0
    drawn = jax.random.normal(rng, extent, jnp.float32) * scale * factor_of
    return jnp.minimum(jnp.maximum(drawn, -limit), limit).astype(dtype)


def setup_inputs(seed: int = 0) -> dict:
    streams_of = jax.random.split(jax.random.key(seed), 8)
    tokens = bell_draw(streams_of[0], (LEVELS, NLAT, NLON, C), 1.0, 6.0, ((0, 2), (1, 8), (2, 32)))
    cotangent = bell_draw(streams_of[1], (LEVELS, NLAT, NLON, C), 1.0, 6.0, ((0, 2), (1, 8), (2, 32)))
    w_qkv = draw_w_qkv(jax.random.fold_in(streams_of[7], 71), 0)
    w_proj = bell_draw(streams_of[3], (C, C), (2.0 / C ** 0.5), 0.609375)
    bias_table = bell_draw(streams_of[4], (TYPES, HEADS, POS), 1.0, 5.0, ((0, 8),), jnp.float32)
    bias_index = plant(jax.random.randint(streams_of[5], (TYPES, WIN, WIN), 0, POS), jax.random.fold_in(streams_of[5], 1), 0, POS - 1).astype(jnp.int32)
    region_ids = plant(jax.random.randint(streams_of[6], (NLAT, NLON), 0, 3), jax.random.fold_in(streams_of[6], 1), 0, 2).astype(jnp.int32)
    return dict(tokens=tokens, cotangent=cotangent, w_qkv=w_qkv, w_proj=w_proj, bias_table=bias_table, bias_index=bias_index, region_ids=region_ids)


def roll_in(field):
    return jnp.roll(field, (-(WLAT // 2), -(WLON // 2)), axis=(1, 2))

def roll_out(field):
    return jnp.roll(field, (WLAT // 2, WLON // 2), axis=(1, 2))

def to_windows(field):
    levels, rows, columns, width = field.shape
    shaped = field.reshape(levels // WLEV, WLEV, rows // WLAT, WLAT, columns // WLON, WLON, width)
    shaped = shaped.transpose(2, 0, 4, 1, 3, 5, 6)
    return shaped.reshape(rows // WLAT, levels // WLEV * (columns // WLON), WIN, width)

def from_windows(blocks, levels, columns):
    types_here, count, win_size, width = blocks.shape
    shaped = blocks.reshape(types_here, levels // WLEV, columns // WLON, WLEV, WLAT, WLON, width)
    shaped = shaped.transpose(1, 3, 0, 4, 2, 5, 6)
    return shaped.reshape(levels, types_here * WLAT, columns, width)

def region_windows(region, level_windows):
    rows, columns = region.shape
    shaped = region.reshape(rows // WLAT, WLAT, columns // WLON, WLON).transpose(0, 2, 1, 3)
    shaped = shaped.reshape(rows // WLAT, columns // WLON, WLAT * WLON)
    shaped = jnp.tile(shaped, (1, 1, WLEV))
    shaped = jnp.broadcast_to(shaped[:, None], (rows // WLAT, level_windows, columns // WLON, WIN))
    return shaped.reshape(rows // WLAT, level_windows * (columns // WLON), WIN)

def window_pass(windows, cot_windows, index_table, bias_rows, region_rows, w_qkv, w_proj):
    count, win_size, width = windows.shape
    heads = bias_rows.shape[0]
    head_size = width // heads
    factor = head_size ** (-0.5)
    flat = windows.reshape(count * win_size, width).astype(jnp.float32)
    center = flat - lax.optimization_barrier(jnp.mean(flat, axis=-1, keepdims=True))
    inverse = lax.rsqrt(lax.optimization_barrier(jnp.mean(center * center, axis=-1, keepdims=True)) + 1e-05)
    unit_rows = center * inverse
    normed = unit_rows.astype(jnp.bfloat16)
    packed = jnp.dot(normed, w_qkv, preferred_element_type=jnp.float32).astype(jnp.bfloat16)
    packed = packed.reshape(count, win_size, 3, heads, head_size)
    query_rows = packed[:, :, 0].astype(jnp.float32)
    key_rows = packed[:, :, 1].astype(jnp.float32)
    value_rows = packed[:, :, 2].astype(jnp.float32)
    scores = jnp.einsum('bihd,bjhd->bhij', query_rows, key_rows) * factor
    scores = scores + jnp.take(bias_rows, index_table, axis=1)[None]
    allowed = (region_rows[:, :, None] == region_rows[:, None, :])[:, None]
    scores = jnp.where(allowed, scores, -1e+30)
    top = lax.optimization_barrier(jnp.max(scores, axis=-1, keepdims=True))
    expo = jnp.exp(scores - top)
    probs = expo / lax.optimization_barrier(jnp.sum(expo, axis=-1, keepdims=True))
    probs_b = probs.astype(jnp.bfloat16).astype(jnp.float32)
    mixed = jnp.einsum('bhij,bjhd->bihd', probs_b, value_rows).astype(jnp.bfloat16)
    mixed = mixed.reshape(count * win_size, width)
    branch = jnp.dot(mixed, w_proj, preferred_element_type=jnp.float32).astype(jnp.bfloat16)
    cot_flat = cot_windows.reshape(count * win_size, width)
    grad_proj = jnp.einsum('tc,td->cd', mixed.astype(jnp.float32), cot_flat.astype(jnp.float32))
    grad_mixed = jnp.dot(cot_flat, w_proj.T, preferred_element_type=jnp.float32).astype(jnp.bfloat16)
    grad_mixed = grad_mixed.reshape(count, win_size, heads, head_size).astype(jnp.float32)
    grad_probs = jnp.einsum('bihd,bjhd->bhij', grad_mixed, value_rows)
    grad_value = jnp.einsum('bhij,bihd->bjhd', probs_b, grad_mixed).astype(jnp.bfloat16)
    grad_scores = probs * (grad_probs - lax.optimization_barrier(jnp.sum(probs * grad_probs, axis=-1, keepdims=True)))
    summed = lax.optimization_barrier(jnp.sum(grad_scores, axis=0)).reshape(heads, win_size * win_size)
    grad_bias = jax.ops.segment_sum(summed.T, index_table.reshape(-1), num_segments=bias_rows.shape[1]).T
    scaled = (grad_scores * factor).astype(jnp.bfloat16).astype(jnp.float32)
    grad_query = jnp.einsum('bhij,bjhd->bihd', scaled, key_rows).astype(jnp.bfloat16)
    grad_key = jnp.einsum('bhij,bihd->bjhd', scaled, query_rows).astype(jnp.bfloat16)
    grad_packed = jnp.stack([grad_query, grad_key, grad_value], 2).reshape(count * win_size, 3 * width)
    grad_qkv = jnp.einsum('tc,te->ce', normed.astype(jnp.float32), grad_packed.astype(jnp.float32))
    grad_normed = jnp.dot(grad_packed, w_qkv.T, preferred_element_type=jnp.float32)
    grad_rows = inverse * (grad_normed - lax.optimization_barrier(jnp.mean(grad_normed, axis=-1, keepdims=True)) - unit_rows * lax.optimization_barrier(jnp.mean(grad_normed * unit_rows, axis=-1, keepdims=True)))
    grad_rows = grad_rows.astype(jnp.bfloat16).reshape(count, win_size, width)
    return (branch.reshape(count, win_size, width), grad_rows, grad_qkv, grad_proj, grad_bias)

def reference(tokens, cotangent, w_qkv, w_proj, bias_table, bias_index, region_ids):
    levels, rows, columns, width = tokens.shape
    windows = to_windows(roll_in(tokens))
    cot_windows = to_windows(roll_in(cotangent))
    regions = region_windows(region_ids, levels // WLEV)

    def one_type(carry, items):
        window_rows, cot_rows, index_table, bias_rows, region_rows = items
        branch, grad_rows, part_qkv, part_proj, grad_bias = window_pass(window_rows, cot_rows, index_table, bias_rows, region_rows, w_qkv, w_proj)
        return ((carry[0] + part_qkv, carry[1] + part_proj), (branch, grad_rows, grad_bias))
    start = (jnp.zeros((width, 3 * width), jnp.float32), jnp.zeros((width, width), jnp.float32))
    (qkv_sum, proj_sum), (branch, grad_rows, grad_table) = lax.scan(one_type, start, (windows, cot_windows, bias_index, bias_table, regions))
    norm_factor = lax.rsqrt(jnp.asarray(TOKENS, jnp.float32))
    block_out = (tokens.astype(jnp.float32) + roll_out(from_windows(branch, levels, columns)).astype(jnp.float32)).astype(jnp.bfloat16)
    grad_tokens = (cotangent.astype(jnp.float32) + roll_out(from_windows(grad_rows, levels, columns)).astype(jnp.float32)).astype(jnp.bfloat16)
    return (block_out, grad_tokens, qkv_sum * norm_factor, proj_sum * norm_factor, grad_table)
```

```python
import functools
import math

import jax
import jax.numpy as jnp
import numpy as np
from jax import lax
from jax.experimental import pallas as pl
from jax.experimental.pallas import tpu as pltpu

F32 = jnp.float32
BF16 = jnp.bfloat16
HEADS = 12
WIN = 144
WIDTH = 384
POS = 3312
FACTOR = 32 ** (-0.5)


def dot(a, b):
    return lax.dot_general(a, b, (((1,), (0,)), ((), ())), preferred_element_type=F32)


def dot_nt(a, b):
    return lax.dot_general(a, b, (((1,), (1,)), ((), ())), preferred_element_type=F32)


def pack_tail(block):
    rows = []
    for q in range(3):
        parts = []
        for b in range(8):
            at = 64 * q + 8 * b
            if at < WIN:
                parts.append(block[at:at + 8, :])
            else:
                parts.append(jnp.full((8, 16), -1, block.dtype))
        rows.append(jnp.concatenate(parts, 1))
    return jnp.concatenate(rows, 0)


def compute_kernel(x_ref, c_ref, wq_ref, wp_ref, tab_ref, idx_ref, regc_ref, regr_ref,
                   branch_ref, rows_ref, g_ref, tgrad_ref,
                   tab_s, idx_s, tail_s, bias_s, qkv_s, qkvt_s, gm_s, gmt_s, mixt_s, gqt_s, gp_s,
                   unit_s, inv_s, normt_s, gs_s, acc_s):
    tab_s[...] = jnp.zeros_like(tab_s)
    tab_s[0:HEADS, 0:POS] = tab_ref[...]
    index_t = idx_ref[...].T
    idx_s[0:WIN, :] = index_t[:, 0:128]
    idx_s[WIN:168, :] = pack_tail(index_t[:, 128:144])

    def look_up(r, store):
        at = pl.multiple_of(r * 8, 8)
        entry = idx_s[pl.ds(at, 8), :]
        low = jnp.bitwise_and(entry, 127)
        high = jnp.right_shift(entry, 7)
        found = [jnp.zeros((8, 128), F32) for _ in range(HEADS)]
        for k in range(26):
            here = high == k
            for h in range(HEADS):
                line = jnp.broadcast_to(tab_s[h:h + 1, 128 * k:128 * k + 128], (8, 128))
                got = jnp.take_along_axis(line, low, axis=1, mode="promise_in_bounds")
                found[h] = jnp.where(here, got, found[h])
        for h in range(HEADS):
            store(h, at, found[h])

    def main_rows(r, carry):
        def store(h, at, value):
            bias_s[h, pl.ds(at, 8), 0:128] = value
        look_up(r, store)
        return carry

    def tail_rows(r, carry):
        def store(h, at, value):
            tail_s[h, pl.ds(pl.multiple_of(at - WIN, 8), 8), :] = value
        look_up(r, store)
        return carry

    lax.fori_loop(0, 18, main_rows, 0)
    lax.fori_loop(18, 21, tail_rows, 0)

    def spread(h, carry):
        for at in range(0, WIN, 8):
            q, b = at // 64, at % 64 // 8
            bias_s[h, at:at + 8, 128:144] = tail_s[h, 8 * q:8 * q + 8, 16 * b:16 * b + 16]
        return carry

    lax.fori_loop(0, HEADS, spread, 0)

    wq = wq_ref[...]
    wp = wp_ref[...]
    flat = x_ref[...].astype(F32)
    center = flat - jnp.mean(flat, axis=-1, keepdims=True)
    inverse = lax.rsqrt(jnp.mean(center * center, axis=-1, keepdims=True) + 1e-05)
    unit = center * inverse
    unit_s[...] = unit
    inv_s[...] = jnp.broadcast_to(inverse, inv_s.shape)
    normed = unit.astype(BF16)
    packed = dot(normed, wq).astype(BF16)
    cot = c_ref[...]
    gm_s[...] = dot_nt(cot, wp).astype(BF16)
    for w in range(2):
        at = slice(WIN * w, WIN * w + WIN)
        qkv_s[w] = packed[at]
        qkvt_s[w] = packed[at].T
        normt_s[w] = normed[at].T
        gmt_s[w] = dot_nt(wp, cot[at]).astype(BF16)

    allowed = [regc_ref[w][:, 0:1] == regr_ref[w][0:1, :] for w in range(2)]
    lane = lax.broadcasted_iota(jnp.int32, (WIN, 128), 1)
    line_of = lax.broadcasted_iota(jnp.int32, (128, WIN), 0)
    for r in range(168):
        pass
    gs_s[...] = jnp.zeros_like(gs_s)

    def group(g, carry):
        off = pl.multiple_of(g * 128, 128)
        keys = [[None] * 2 for _ in range(4)]
        grad_key = [None, None]
        grad_value = [None, None]
        for a in range(4):
            h = g * 4 + a
            mine = (line_of >= 32 * a) & (line_of < 32 * a + 32)
            mine_lane = (lane >= 32 * a) & (lane < 32 * a + 32)
            total = None
            bias = bias_s[h]
            for w in range(2):
                q = qkv_s[w, :, pl.ds(off, 128)]
                k = qkv_s[w, :, pl.ds(off + 384, 128)]
                v = qkv_s[w, :, pl.ds(off + 768, 128)]
                qt = qkvt_s[w, pl.ds(off, 128), :]
                gmt = gmt_s[w, pl.ds(off, 128), :]
                here = pl.multiple_of(off + 32 * a, 32)
                kt = qkvt_s[w, pl.ds(384 + here, 32), :]
                vt = qkvt_s[w, pl.ds(768 + here, 32), :]
                gm = gm_s[pl.ds(WIN * w, WIN), pl.ds(off, 128)]
                zero = jnp.zeros((), BF16)
                s = dot(k, jnp.where(mine, qt, zero)) * FACTOR + bias
                s = jnp.where(allowed[w], s, -1e30)
                e = jnp.exp(s - jnp.max(s, axis=0, keepdims=True))
                p = e * (1.0 / jnp.sum(e, axis=0, keepdims=True))
                pb = p.astype(BF16)
                mixt_s[w, pl.ds(here, 32), :] = dot(vt, pb).astype(BF16)
                gpr = dot(v, jnp.where(mine, gmt, zero))
                gv = dot(pb, gm)
                gs = p * (gpr - jnp.sum(p * gpr, axis=0, keepdims=True))
                sc = (gs * FACTOR).astype(BF16)
                gqt_s[w, pl.ds(here, 32), :] = dot(kt, sc).astype(BF16)
                gk = dot(sc, q)
                grad_key[w] = gk if a == 0 else jnp.where(mine_lane, gk, grad_key[w])
                grad_value[w] = gv if a == 0 else jnp.where(mine_lane, gv, grad_value[w])
                total = gs if w == 0 else total + gs
            gs_s[0:WIN, pl.ds(h, 1), :] = total[:, 0:128].reshape(WIN, 1, 128)
            gs_s[WIN:168, pl.ds(h, 1), :] = pack_tail(total[:, 128:144]).reshape(24, 1, 128)
        for w in range(2):
            rows = slice(WIN * w, WIN * w + WIN)
            gp_s[rows, pl.ds(off + 384, 128)] = grad_key[w].astype(BF16)
            gp_s[rows, pl.ds(off + 768, 128)] = grad_value[w].astype(BF16)
        return carry

    lax.fori_loop(0, 3, group, 0)

    for w in range(2):
        rows = slice(WIN * w, WIN * w + WIN)
        gp_s[rows, 0:384] = gqt_s[w].T
        branch_ref[rows, :] = dot(mixt_s[w].T, wp).astype(BF16)
    gn = dot_nt(gp_s[...], wq)
    unit = unit_s[...]
    rows_ref[...] = (inv_s[:, 0:1] * (
        gn - jnp.mean(gn, axis=-1, keepdims=True)
        - unit * jnp.mean(gn * unit, axis=-1, keepdims=True))).astype(BF16)
    for half in range(2):
        part = [dot(normt_s[w], gp_s[WIN * w:WIN * w + WIN, 576 * half:576 * half + 576]) for w in range(2)]
        g_ref[half, :, 0:576] = part[0] + part[1]
        part = [dot(mixt_s[w], c_ref[WIN * w:WIN * w + WIN, 192 * half:192 * half + 192]) for w in range(2)]
        g_ref[half, :, 576:768] = part[0] + part[1]

    acc_s[...] = jnp.zeros_like(acc_s)
    low_of = lax.broadcasted_iota(jnp.int32, (256, 128), 0)

    def pairs(r, carry):
        entry = idx_s[pl.ds(pl.multiple_of(r * 8, 8), 8), :]
        low = jnp.bitwise_and(entry, 255)
        high = jnp.right_shift(entry, 8)
        lefts = []
        rights = []
        for s in range(8):
            value = gs_s[r * 8 + s]
            lefts.append(jnp.concatenate(
                [jnp.where(high[s:s + 1, :] == k, value, 0.0).astype(BF16) for k in range(13)], 0))
            rights.append(jnp.where(low[s:s + 1, :] == low_of, 1.0, 0.0).astype(BF16))
        acc_s[...] += dot_nt(jnp.concatenate(lefts, 1), jnp.concatenate(rights, 1))
        return carry

    lax.fori_loop(0, 21, pairs, 0)
    tgrad_ref[...] = jnp.zeros_like(tgrad_ref)
    for o in range(13):
        tgrad_ref[24 * o:24 * o + 12, :] = acc_s[16 * o:16 * o + 12, 0:128]
        tgrad_ref[24 * o + 12:24 * o + 24, :] = acc_s[16 * o:16 * o + 12, 128:256]


def compute(x, c, wq, wp, tab, idx, reg):
    regc = jnp.broadcast_to(reg[:, :, None], (2, WIN, 128))
    regr = jnp.broadcast_to(reg[:, None, :], (2, 8, WIN))
    return pl.pallas_call(
        compute_kernel,
        out_shape=[
            jax.ShapeDtypeStruct((288, 384), BF16),
            jax.ShapeDtypeStruct((288, 384), BF16),
            jax.ShapeDtypeStruct((2, 384, 768), F32),
            jax.ShapeDtypeStruct((384, 128), F32),
        ],
        scratch_shapes=[
            pltpu.VMEM((16, 3328), F32),
            pltpu.VMEM((168, 128), jnp.int32),
            pltpu.VMEM((12, 24, 128), F32),
            pltpu.VMEM((12, 144, 144), F32),
            pltpu.VMEM((2, 144, 1152), BF16),
            pltpu.VMEM((2, 1152, 144), BF16),
            pltpu.VMEM((288, 384), BF16),
            pltpu.VMEM((2, 384, 144), BF16),
            pltpu.VMEM((2, 384, 144), BF16),
            pltpu.VMEM((2, 384, 144), BF16),
            pltpu.VMEM((288, 1152), BF16),
            pltpu.VMEM((288, 384), F32),
            pltpu.VMEM((288, 128), F32),
            pltpu.VMEM((2, 384, 144), BF16),
            pltpu.VMEM((168, 16, 128), F32),
            pltpu.VMEM((208, 256), F32),
        ],
        compiler_params=pltpu.CompilerParams(vmem_limit_bytes=48 * 1024 * 1024),
        name="window_math",
    )(x, c, wq, wp, tab, idx, regc, regr)


PIECES = ((0, 112), (112, 48), (160, 48))
MESH = pl.DeviceIdType.MESH


@functools.lru_cache(None)
def permutations():
    place = {}
    for l in range(2):
        for r in range(3):
            for c in range(6, 24):
                place[l, r, c] = l * 54 + r * 18 + c - 6
        for r in range(3, 6):
            for c in range(6):
                place[l, r, c] = 112 + l * 18 + (r - 3) * 6 + c
        for r in range(3):
            for c in range(6):
                place[l, r, c] = 160 + l * 18 + r * 6 + c
    send = np.zeros((208, 288), np.float32)
    for (l, r, c), at in place.items():
        send[at, l * 144 + r * 24 + c] = 1
    own = np.zeros((288, 288), np.float32)
    recv = np.zeros((288, 208), np.float32)
    for w in range(2):
        for l in range(2):
            for r in range(6):
                for c in range(12):
                    row = w * 144 + l * 72 + r * 12 + c
                    at, col = r + 3, 12 * w + c + 6
                    if at < 6 and col < 24:
                        own[row, l * 144 + at * 24 + col] = 1
                    else:
                        recv[row, place[l, at % 6, col % 24]] = 1
    return send, own, recv


def step(index, by, count):
    return lax.rem(index + (by + count), count)


def halo_in_kernel(nlat, nlon, x_ref, c_ref, take_ref, own_ref, put_ref, xo_ref, co_ref,
                   send, recv, send_sem, recv_sem):
    lat, lon = lax.axis_index("lat"), lax.axis_index("lon")
    before = [{"lat": step(lat, -1, nlat), "lon": lon}, {"lat": lat, "lon": step(lon, -1, nlon)},
              {"lat": step(lat, -1, nlat), "lon": step(lon, -1, nlon)}]
    after = [{"lat": step(lat, 1, nlat), "lon": lon}, {"lat": lat, "lon": step(lon, 1, nlon)},
             {"lat": step(lat, 1, nlat), "lon": step(lon, 1, nlon)}]
    barrier = pltpu.get_barrier_semaphore()
    for device in after:
        pl.semaphore_signal(barrier, inc=1, device_id=device, device_id_type=MESH)
    for f, ref in enumerate((x_ref, c_ref)):
        send[f] = dot(take_ref[...], ref[...]).astype(BF16)
    pl.semaphore_wait(barrier, 3)
    copies = []
    for f in range(2):
        for n, (at, size) in enumerate(PIECES):
            copy = pltpu.make_async_remote_copy(
                src_ref=send.at[f, pl.ds(at, size)], dst_ref=recv.at[f, pl.ds(at, size)],
                send_sem=send_sem.at[3 * f + n], recv_sem=recv_sem.at[3 * f + n],
                device_id=before[n], device_id_type=MESH)
            copy.start()
            copies.append(copy)
    mine = [dot(own_ref[...], ref[...]) for ref in (x_ref, c_ref)]
    for f, ref in enumerate((xo_ref, co_ref)):
        for copy in copies[3 * f:3 * f + 3]:
            copy.wait()
        ref[...] = (mine[f] + dot(put_ref[...], recv[f])).astype(BF16)


def halo_in(nlat, nlon, x, c, take, own, put):
    return pl.pallas_call(
        functools.partial(halo_in_kernel, nlat, nlon),
        out_shape=[jax.ShapeDtypeStruct((288, 384), BF16)] * 2,
        scratch_shapes=[
            pltpu.VMEM((2, 208, 384), BF16),
            pltpu.VMEM((2, 208, 384), BF16),
            pltpu.SemaphoreType.DMA((6,)),
            pltpu.SemaphoreType.DMA((6,)),
        ],
        compiler_params=pltpu.CompilerParams(
            collective_id=0, has_side_effects=True, vmem_limit_bytes=32 * 1024 * 1024),
        name="halo_in",
    )(x, c, take, own, put)


def finish_kernel(nlat, nlon, norm, x_ref, c_ref, branch_ref, rows_ref, g_ref, tpart_ref,
                  take_ref, own_ref, put_ref, xo_ref, co_ref, gq_ref, gp_ref, to_ref,
                  send, recv, gsend, gcore, lat_send, lat_recv, turn, turned, ypart, ysend, yrecv,
                  zpart, zrecv, trecv, tsum, tzrecv, tfull,
                  halo_ss, halo_rs, core_ss, core_rs, lat_ss, lat_rs, y_ss, y_rs, z_ss, z_rs,
                  t_ss, t_rs, tz_ss, tz_rs, tg_ss, tg_rs):
    nz = nlon // 8
    lev, lat, lon = lax.axis_index("lev"), lax.axis_index("lat"), lax.axis_index("lon")
    z, y = lon // 8, lax.rem(lon, 8)
    owner = lev * 8 + y

    def at_owner(o):
        return {"lev": o // 8, "lat": lat, "lon": z * 8 + lax.rem(o, 8)}

    core_peer = {"lev": 1 - lev, "lat": lat, "lon": lon}
    lat_peers = [{"lev": lev, "lat": step(lat, d, nlat), "lon": lon} for d in range(1, nlat)]
    y_peers = [{"lev": lev, "lat": lat, "lon": z * 8 + step(y, d, 8)} for d in range(1, 8)]
    z_peers = [{"lev": lev, "lat": lat, "lon": step(z, d, nz) * 8 + y} for d in range(1, nz)]
    owners = [at_owner(step(owner, d, 16)) for d in range(1, 16)]
    after = [{"lev": lev, "lat": step(lat, 1, nlat), "lon": lon},
             {"lev": lev, "lat": lat, "lon": step(lon, 1, nlon)},
             {"lev": lev, "lat": step(lat, 1, nlat), "lon": step(lon, 1, nlon)}]
    before = [{"lev": lev, "lat": lat, "lon": step(lon, -1, nlon)},
              {"lev": lev, "lat": step(lat, -1, nlat), "lon": step(lon, -1, nlon)}]
    barrier = pltpu.get_barrier_semaphore()
    greet = owners + lat_peers + z_peers + after[1:] + before
    for device in greet:
        pl.semaphore_signal(barrier, inc=1, device_id=device, device_id_type=MESH)
    gsend[...] = g_ref[1 - lev].astype(BF16)
    for f, ref in enumerate((branch_ref, rows_ref)):
        send[f] = dot(take_ref[...], ref[...]).astype(BF16)
    pl.semaphore_wait(barrier, len(greet))

    def push(src, dst, ss, rs, device):
        copy = pltpu.make_async_remote_copy(
            src_ref=src, dst_ref=dst, send_sem=ss, recv_sem=rs, device_id=device, device_id_type=MESH)
        copy.start()
        return copy

    lat_rows = [pl.ds(pl.multiple_of(48 * step(lat, d, nlat), 48), 48) for d in range(1, nlat + 1)]
    core = [push(gsend.at[rows], gcore.at[rows], core_ss.at[n], core_rs.at[n], core_peer)
            for n, rows in enumerate(lat_rows)]
    halo = [push(send.at[f, pl.ds(at, size)], recv.at[f, pl.ds(at, size)],
                 halo_ss.at[3 * f + n], halo_rs.at[3 * f + n], after[n])
            for f in range(2) for n, (at, size) in enumerate(PIECES)]
    table = [push(tpart_ref.at[pl.ds(pl.multiple_of(24 * step(owner, d, 16), 24), 24)],
                  trecv.at[d - 1], t_ss.at[d - 1], t_rs.at[d - 1], owners[d - 1])
             for d in range(1, 16)]

    over_lat = []
    for n in range(nlat - 1):
        core[n].wait()
        lat_send[n] = (g_ref[lev, lat_rows[n], :] + gcore[lat_rows[n], :].astype(F32)).astype(BF16)
        over_lat.append(push(lat_send.at[n], lat_recv.at[n], lat_ss.at[n], lat_rs.at[n], lat_peers[n]))
    core[nlat - 1].wait()
    total = g_ref[lev, lat_rows[-1], :] + gcore[lat_rows[-1], :].astype(F32)

    mine = tpart_ref[pl.ds(pl.multiple_of(24 * owner, 24), 24), :]
    for n in range(15):
        table[n].wait()
        mine = mine + trecv[n]
    tsum[0] = mine
    over_z = [push(tsum.at[0], tzrecv.at[n], tz_ss.at[n], tz_rs.at[n], z_peers[n]) for n in range(nz - 1)]

    for f, (base, ref, out) in enumerate(((x_ref, branch_ref, xo_ref), (c_ref, rows_ref, co_ref))):
        for copy in halo[3 * f:3 * f + 3]:
            copy.wait()
        rolled = dot(own_ref[...], ref[...]) + dot(put_ref[...], recv[f])
        out[...] = (base[...].astype(F32) + rolled).astype(BF16)

    for n in range(nz - 1):
        over_z[n].wait()
        mine = mine + tzrecv[n]
    tsum[1] = mine
    own_block = pl.ds(pl.multiple_of(24 * owner, 24), 24)
    gathered = [push(tsum.at[1], tfull.at[own_block], tg_ss.at[n], tg_rs.at[n], owners[n])
                for n in range(15)]

    for n in range(nlat - 1):
        over_lat[n].wait()
        total = total + lat_recv[n].astype(F32)

    turn[...] = jnp.zeros_like(turn)
    turn[0:48, :] = total
    turn[64:112, :] = total
    turned[...] = turn[...].T
    first = lax.broadcasted_iota(jnp.int32, (24, 128), 1) < 64
    for to in range(8):
        for p in range(nz // 2):
            a, b = 16 * p + to, 16 * p + 8 + to
            ypart[to, 24 * p:24 * p + 18, :] = jnp.where(
                first[0:18], turned[18 * a:18 * a + 18, :], turned[18 * b:18 * b + 18, :])
            ypart[to, 24 * p + 18:24 * p + 24, :] = jnp.where(
                first[0:6], turned[576 + 6 * a:576 + 6 * a + 6, :], turned[576 + 6 * b:576 + 6 * b + 6, :])
    ysend[...] = ypart[...].astype(BF16)
    over_y = [push(ysend.at[step(y, d, 8)], yrecv.at[d - 1], y_ss.at[d - 1], y_rs.at[d - 1], y_peers[d - 1])
              for d in range(1, 8)]
    total = ypart[y]
    for n in range(7):
        over_y[n].wait()
        total = total + yrecv[n].astype(F32)
    zpart[...] = total
    last = [push(zpart.at[pl.ds(pl.multiple_of(24 * (step(z, d, nz) // 2), 24), 24)],
                 zrecv.at[d - 1], z_ss.at[d - 1], z_rs.at[d - 1], z_peers[d - 1])
            for d in range(1, nz)]

    tfull[own_block, :] = mine
    for n in range(15):
        gathered[n].wait()
    for o in range(13):
        to_ref[:, 256 * o:256 * o + 128] = tfull[24 * o:24 * o + 12, :]
        width = min(128, POS - 256 * o - 128)
        to_ref[:, 256 * o + 128:256 * o + 128 + width] = tfull[24 * o + 12:24 * o + 24, 0:width]

    total = zpart[pl.ds(pl.multiple_of(24 * (z // 2), 24), 24), :]
    for n in range(nz - 1):
        last[n].wait()
        total = total + zrecv[n]
    total = jnp.where(lax.rem(z, 2) == 0, total[:, 0:48], total[:, 64:112]) * norm
    gq_ref[...] = total[0:18]
    gp_ref[...] = total[18:24]


def finish(nlat, nlon, norm, x, c, branch, rows, g, tpart, take, own, put):
    nz = nlon // 8
    sem = pltpu.SemaphoreType.DMA
    return pl.pallas_call(
        functools.partial(finish_kernel, nlat, nlon, norm),
        out_shape=[
            jax.ShapeDtypeStruct((288, 384), BF16),
            jax.ShapeDtypeStruct((288, 384), BF16),
            jax.ShapeDtypeStruct((18, 48), F32),
            jax.ShapeDtypeStruct((6, 48), F32),
            jax.ShapeDtypeStruct((HEADS, POS), F32),
        ],
        scratch_shapes=[
            pltpu.VMEM((2, 208, 384), BF16),
            pltpu.VMEM((2, 208, 384), BF16),
            pltpu.VMEM((384, 768), BF16),
            pltpu.VMEM((384, 768), BF16),
            pltpu.VMEM((nlat - 1, 48, 768), BF16),
            pltpu.VMEM((nlat - 1, 48, 768), BF16),
            pltpu.VMEM((128, 768), F32),
            pltpu.VMEM((768, 128), F32),
            pltpu.VMEM((8, 48, 128), F32),
            pltpu.VMEM((8, 48, 128), BF16),
            pltpu.VMEM((7, 48, 128), BF16),
            pltpu.VMEM((48, 128), F32),
            pltpu.VMEM((nz - 1, 24, 128), F32),
            pltpu.VMEM((15, 24, 128), F32),
            pltpu.VMEM((2, 24, 128), F32),
            pltpu.VMEM((nz - 1, 24, 128), F32),
            pltpu.VMEM((384, 128), F32),
            sem((6,)), sem((6,)), sem((nlat,)), sem((nlat,)), sem((nlat - 1,)), sem((nlat - 1,)),
            sem((7,)), sem((7,)), sem((nz - 1,)), sem((nz - 1,)),
            sem((15,)), sem((15,)), sem((nz - 1,)), sem((nz - 1,)), sem((15,)), sem((15,)),
        ],
        compiler_params=pltpu.CompilerParams(
            collective_id=1, has_side_effects=True, vmem_limit_bytes=48 * 1024 * 1024),
        name="finish",
    )(x, c, branch, rows, g, tpart, take, own, put)


def body(tokens, cotangent, w_qkv, w_proj, bias_table, bias_index, region_ids):
    levels, rows, columns, width = tokens.shape
    nlev, nlat, nlon = lax.axis_size("lev"), lax.axis_size("lat"), lax.axis_size("lon")
    norm = 1.0 / math.sqrt(levels * nlev * rows * nlat * columns * nlon)
    send, own, recv = permutations()
    send, own, recv, send_t, own_t, recv_t = [
        jnp.asarray(m, BF16) for m in (send, own, recv, send.T, own.T, recv.T)]
    x = tokens.reshape(288, width)
    c = cotangent.reshape(288, width)
    regions = jnp.tile(region_ids.reshape(6, 2, 12).transpose(1, 0, 2).reshape(2, 72), (1, 2))
    xw, cw = halo_in(nlat, nlon, x, c, send, own, recv)
    branch, grad_rows, g, tpart = compute(
        xw, cw, w_qkv, w_proj, bias_table[0], bias_index[0], regions)
    block_out, grad_tokens, gq, gp, table = finish(
        nlat, nlon, norm, x, c, branch, grad_rows, g, tpart, recv_t, own_t, send_t)
    return (block_out.reshape(tokens.shape), grad_tokens.reshape(tokens.shape), gq.T, gp.T, table[None])


def solution(mesh):
    return jax.shard_map(
        body,
        mesh=mesh,
        in_specs=(
            jax.P("lev", "lat", "lon", None),
            jax.P("lev", "lat", "lon", None),
            jax.P(),
            jax.P(),
            jax.P("lat", None, None),
            jax.P("lat", None, None),
            jax.P("lat", "lon"),
        ),
        out_specs=(
            jax.P("lev", "lat", "lon", None),
            jax.P("lev", "lat", "lon", None),
            jax.P("lat", ("lev", "lon")),
            jax.P("lat", ("lev", "lon")),
            jax.P("lat", None, None),
        ),
        check_vma=False,
    )
```

```python
import functools
import math

import jax
import jax.numpy as jnp
import numpy as np
from jax import lax
from jax.experimental import pallas as pl
from jax.experimental.pallas import tpu as pltpu

F32 = jnp.float32
BF16 = jnp.bfloat16
HEADS = 12
WIN = 144
WIDTH = 384
POS = 3312
FACTOR = 32 ** (-0.5)


def dot(a, b):
    return lax.dot_general(a, b, (((1,), (0,)), ((), ())), preferred_element_type=F32)


def dot_nt(a, b):
    return lax.dot_general(a, b, (((1,), (1,)), ((), ())), preferred_element_type=F32)


def pack_tail(block):
    rows = []
    for q in range(3):
        parts = []
        for b in range(8):
            at = 64 * q + 8 * b
            if at < WIN:
                parts.append(block[at:at + 8, :])
            else:
                parts.append(jnp.full((8, 16), -1, block.dtype))
        rows.append(jnp.concatenate(parts, 1))
    return jnp.concatenate(rows, 0)


PIECES = ((0, 112), (112, 48), (160, 48))
MESH = pl.DeviceIdType.MESH


@functools.lru_cache(None)
def permutations():
    place = {}
    for l in range(2):
        for r in range(3):
            for c in range(6, 24):
                place[l, r, c] = l * 54 + r * 18 + c - 6
        for r in range(3, 6):
            for c in range(6):
                place[l, r, c] = 112 + l * 18 + (r - 3) * 6 + c
        for r in range(3):
            for c in range(6):
                place[l, r, c] = 160 + l * 18 + r * 6 + c
    send = np.zeros((208, 288), np.float32)
    for (l, r, c), at in place.items():
        send[at, l * 144 + r * 24 + c] = 1
    own = np.zeros((288, 288), np.float32)
    recv = np.zeros((288, 208), np.float32)
    for w in range(2):
        for l in range(2):
            for r in range(6):
                for c in range(12):
                    row = w * 144 + l * 72 + r * 12 + c
                    at, col = r + 3, 12 * w + c + 6
                    if at < 6 and col < 24:
                        own[row, l * 144 + at * 24 + col] = 1
                    else:
                        recv[row, place[l, at % 6, col % 24]] = 1
    return send, own, recv


def step(index, by, count):
    return lax.rem(index + (by + count), count)


def block_kernel(nlat, nlon, norm, x_hbm, c_hbm, wq_hbm, wp_hbm, tab_hbm, idx_hbm, reg_hbm,
                 take_hbm, own_hbm, put_hbm, take_t_hbm, own_t_hbm, put_t_hbm,
                 xo_ref, co_ref, gq_ref, gp_ref, to_ref,
                 x_ref, c_ref, wq_ref, wp_ref, tab_ref, idx_ref, reg_ref,
                 take_ref, own_ref, put_ref, take_t_ref, own_t_ref, put_t_ref,
                 xw_s, cw_s, idx_s, tail_s, bias_s, qkv_s, qkvt_s, gm_s, gmt_s, mixt_s, gqt_s, gp_s,
                 unit_s, inv_s, normt_s, gs_s, acc_s, branch_s, rows_s, g_s, tpart,
                 send_in, recv_in, send, recv, gsend, gcore, lat_send, lat_recv, turn, turned, ypart, ysend, yrecv,
                 zpart, zrecv, trecv, tsum, tzrecv, tfull,
                 load_sem, in_ss, in_rs, halo_ss, halo_rs, core_ss, core_rs, lat_ss, lat_rs,
                 y_ss, y_rs, z_ss, z_rs, t_ss, t_rs, tz_ss, tz_rs, tg_ss, tg_rs):
    names = ("x", "c", "take", "own", "put", "tab", "idx", "reg", "wq", "wp", "own_t", "take_t", "put_t")
    from_to = ((x_hbm, x_ref), (c_hbm, c_ref), (take_hbm, take_ref), (own_hbm, own_ref), (put_hbm, put_ref),
                (tab_hbm, tab_ref), (idx_hbm, idx_ref), (reg_hbm, reg_ref), (wq_hbm, wq_ref), (wp_hbm, wp_ref),
                (own_t_hbm, own_t_ref), (take_t_hbm, take_t_ref), (put_t_hbm, put_t_ref))
    loads = {}
    for n, (name, (src, dst)) in enumerate(zip(names, from_to)):
        loads[name] = pltpu.make_async_copy(src, dst, load_sem.at[n])
        loads[name].start()

    nz = nlon // 8
    lev, lat, lon = lax.axis_index("lev"), lax.axis_index("lat"), lax.axis_index("lon")
    z, y = lon // 8, lax.rem(lon, 8)
    owner = lev * 8 + y

    def at_owner(o):
        return {"lev": o // 8, "lat": lat, "lon": z * 8 + lax.rem(o, 8)}

    core_peer = {"lev": 1 - lev, "lat": lat, "lon": lon}
    lat_peers = [{"lev": lev, "lat": step(lat, d, nlat), "lon": lon} for d in range(1, nlat)]
    y_peers = [{"lev": lev, "lat": lat, "lon": z * 8 + step(y, d, 8)} for d in range(1, 8)]
    z_peers = [{"lev": lev, "lat": lat, "lon": step(z, d, nz) * 8 + y} for d in range(1, nz)]
    owners = [at_owner(step(owner, d, 16)) for d in range(1, 16)]
    after, before = [
        [{"lev": lev, "lat": step(lat, by, nlat), "lon": lon},
         {"lev": lev, "lat": lat, "lon": step(lon, by, nlon)},
         {"lev": lev, "lat": step(lat, by, nlat), "lon": step(lon, by, nlon)}] for by in (1, -1)]
    barrier = pltpu.get_barrier_semaphore()
    greet = after[1:] + before[1:] + lat_peers + owners + z_peers
    for device in greet:
        pl.semaphore_signal(barrier, inc=1, device_id=device, device_id_type=MESH)

    def push(src, dst, ss, rs, device):
        copy = pltpu.make_async_remote_copy(
            src_ref=src, dst_ref=dst, send_sem=ss, recv_sem=rs, device_id=device, device_id_type=MESH)
        copy.start()
        return copy

    for name in ("x", "c", "take"):
        loads[name].wait()
    for f, ref in enumerate((x_ref, c_ref)):
        send_in[f] = dot(take_ref[...], ref[...]).astype(BF16)
    pl.semaphore_wait(barrier, len(greet))
    arrive = [push(send_in.at[f, pl.ds(at, size)], recv_in.at[f, pl.ds(at, size)],
                   in_ss.at[3 * f + n], in_rs.at[3 * f + n], before[n])
              for f in range(2) for n, (at, size) in enumerate(PIECES)]

    for name in ("tab", "idx"):
        loads[name].wait()
    index_t = idx_ref[...].T
    idx_s[0:WIN, :] = index_t[:, 0:128]
    idx_s[WIN:168, :] = pack_tail(index_t[:, 128:144])

    def look_up(r, store):
        at = pl.multiple_of(r * 8, 8)
        entry = idx_s[pl.ds(at, 8), :]
        low = jnp.bitwise_and(entry, 127)
        high = jnp.right_shift(entry, 7)
        found = [jnp.zeros((8, 128), F32) for _ in range(HEADS)]
        for k in range(26):
            here = high == k
            width = min(128, POS - 128 * k)
            for h in range(HEADS):
                line = tab_ref[h, 0:1, 128 * k:128 * k + width]
                if width < 128:
                    line = jnp.concatenate([line, jnp.zeros((1, 128 - width), F32)], 1)
                line = jnp.broadcast_to(line, (8, 128))
                got = jnp.take_along_axis(line, low, axis=1, mode="promise_in_bounds")
                found[h] = jnp.where(here, got, found[h])
        for h in range(HEADS):
            store(h, at, found[h])

    def main_rows(r, carry):
        def store(h, at, value):
            bias_s[h, pl.ds(at, 8), 0:128] = value
        look_up(r, store)
        return carry

    def tail_rows(r, carry):
        def store(h, at, value):
            tail_s[h, pl.ds(pl.multiple_of(at - WIN, 8), 8), :] = value
        look_up(r, store)
        return carry

    lax.fori_loop(0, 18, main_rows, 0)
    lax.fori_loop(18, 21, tail_rows, 0)

    def spread(h, carry):
        for at in range(0, WIN, 8):
            q, b = at // 64, at % 64 // 8
            bias_s[h, at:at + 8, 128:144] = tail_s[h, 8 * q:8 * q + 8, 16 * b:16 * b + 16]
        return carry

    lax.fori_loop(0, HEADS, spread, 0)
    gs_s[...] = jnp.zeros_like(gs_s)

    loads["reg"].wait()
    region = reg_ref[...].astype(F32).astype(BF16)
    col_of = lax.broadcasted_iota(jnp.int32, (24, WIN), 0)
    place = lax.broadcasted_iota(jnp.int32, (24, WIN), 1)
    row_of = lax.broadcasted_iota(jnp.int32, (6, WIN), 0)
    row_at = lax.rem(lax.broadcasted_iota(jnp.int32, (6, WIN), 1), 72) // 12
    allowed = []
    for w in range(2):
        choose = jnp.where(col_of == lax.rem(place, 12) + 12 * w, 1.0, 0.0).astype(BF16)
        line = jnp.sum(jnp.where(row_of == row_at, dot(region, choose), 0.0), axis=0, keepdims=True)
        down = jnp.broadcast_to(line, (128, WIN)).T
        allowed.append(down[:, 0:1] == line)

    loads["own"].wait()
    loads["put"].wait()
    mine = [dot(own_ref[...], ref[...]) for ref in (x_ref, c_ref)]
    for f, ref in enumerate((xw_s, cw_s)):
        for copy in arrive[3 * f:3 * f + 3]:
            copy.wait()
        ref[...] = (mine[f] + dot(put_ref[...], recv_in[f])).astype(BF16)

    loads["wq"].wait()
    loads["wp"].wait()
    flat = xw_s[...].astype(F32)
    center = flat - jnp.mean(flat, axis=-1, keepdims=True)
    inverse = lax.rsqrt(jnp.mean(center * center, axis=-1, keepdims=True) + 1e-05)
    unit = center * inverse
    unit_s[...] = unit
    inv_s[...] = jnp.broadcast_to(inverse, inv_s.shape)
    normed = unit.astype(BF16)
    packed = dot(normed, wq_ref[...]).astype(BF16)
    cot = cw_s[...]
    gm_s[...] = dot_nt(cot, wp_ref[...]).astype(BF16)
    for w in range(2):
        at = slice(WIN * w, WIN * w + WIN)
        qkv_s[w] = packed[at]
        qkvt_s[w] = packed[at].T
        normt_s[w] = normed[at].T
        gmt_s[w] = dot_nt(wp_ref[...], cot[at]).astype(BF16)

    lane = lax.broadcasted_iota(jnp.int32, (WIN, 128), 1)
    line_of = lax.broadcasted_iota(jnp.int32, (128, WIN), 0)

    def group(g, carry):
        off = pl.multiple_of(g * 128, 128)
        grad_key = [None, None]
        grad_value = [None, None]
        for a in range(4):
            h = g * 4 + a
            own_line = (line_of >= 32 * a) & (line_of < 32 * a + 32)
            own_lane = (lane >= 32 * a) & (lane < 32 * a + 32)
            total = None
            bias = bias_s[h]
            for w in range(2):
                q = qkv_s[w, :, pl.ds(off, 128)]
                k = qkv_s[w, :, pl.ds(off + 384, 128)]
                v = qkv_s[w, :, pl.ds(off + 768, 128)]
                qt = qkvt_s[w, pl.ds(off, 128), :]
                gmt = gmt_s[w, pl.ds(off, 128), :]
                here = pl.multiple_of(off + 32 * a, 32)
                kt = qkvt_s[w, pl.ds(384 + here, 32), :]
                vt = qkvt_s[w, pl.ds(768 + here, 32), :]
                gm = gm_s[pl.ds(WIN * w, WIN), pl.ds(off, 128)]
                zero = jnp.zeros((), BF16)
                s = dot(k, jnp.where(own_line, qt, zero)) * FACTOR + bias
                s = jnp.where(allowed[w], s, -1e30)
                e = jnp.exp(s - jnp.max(s, axis=0, keepdims=True))
                p = e * (1.0 / jnp.sum(e, axis=0, keepdims=True))
                pb = p.astype(BF16)
                mixt_s[w, pl.ds(here, 32), :] = dot(vt, pb).astype(BF16)
                gpr = dot(v, jnp.where(own_line, gmt, zero))
                gv = dot(pb, gm)
                gs = p * (gpr - jnp.sum(p * gpr, axis=0, keepdims=True))
                sc = (gs * FACTOR).astype(BF16)
                gqt_s[w, pl.ds(here, 32), :] = dot(kt, sc).astype(BF16)
                gk = dot(sc, q)
                grad_key[w] = gk if a == 0 else jnp.where(own_lane, gk, grad_key[w])
                grad_value[w] = gv if a == 0 else jnp.where(own_lane, gv, grad_value[w])
                total = gs if w == 0 else total + gs
            gs_s[0:WIN, pl.ds(h, 1), :] = total[:, 0:128].reshape(WIN, 1, 128)
            gs_s[WIN:168, pl.ds(h, 1), :] = pack_tail(total[:, 128:144]).reshape(24, 1, 128)
        for w in range(2):
            rows = slice(WIN * w, WIN * w + WIN)
            gp_s[rows, pl.ds(off + 384, 128)] = grad_key[w].astype(BF16)
            gp_s[rows, pl.ds(off + 768, 128)] = grad_value[w].astype(BF16)
        return carry

    lax.fori_loop(0, 3, group, 0)

    for w in range(2):
        gp_s[WIN * w:WIN * w + WIN, 0:384] = gqt_s[w].T
    for half in range(2):
        part = [dot(normt_s[w], gp_s[WIN * w:WIN * w + WIN, 576 * half:576 * half + 576]) for w in range(2)]
        g_s[half, :, 0:576] = part[0] + part[1]
        part = [dot(mixt_s[w], cw_s[WIN * w:WIN * w + WIN, 192 * half:192 * half + 192]) for w in range(2)]
        g_s[half, :, 576:768] = part[0] + part[1]
    gsend[...] = g_s[1 - lev].astype(BF16)
    lat_rows = [pl.ds(pl.multiple_of(48 * step(lat, d, nlat), 48), 48) for d in range(1, nlat + 1)]
    core = [push(gsend.at[rows], gcore.at[rows], core_ss.at[n], core_rs.at[n], core_peer)
            for n, rows in enumerate(lat_rows)]

    loads["put_t"].wait()
    halo = []

    def halo_out(f, ref):
        send[f] = dot(put_t_ref[...], ref[...]).astype(BF16)
        for n, (at, size) in enumerate(PIECES):
            halo.append(push(send.at[f, pl.ds(at, size)], recv.at[f, pl.ds(at, size)],
                             halo_ss.at[3 * f + n], halo_rs.at[3 * f + n], after[n]))

    for w in range(2):
        branch_s[WIN * w:WIN * w + WIN, :] = dot(mixt_s[w].T, wp_ref[...]).astype(BF16)
    halo_out(0, branch_s)

    over_lat = []
    for n in range(nlat - 1):
        core[n].wait()
        lat_send[n] = (g_s[lev, lat_rows[n], :] + gcore[lat_rows[n], :].astype(F32)).astype(BF16)
        over_lat.append(push(lat_send.at[n], lat_recv.at[n], lat_ss.at[n], lat_rs.at[n], lat_peers[n]))
    core[nlat - 1].wait()

    gn = dot_nt(gp_s[...], wq_ref[...])
    unit = unit_s[...]
    rows_s[...] = (inv_s[:, 0:1] * (
        gn - jnp.mean(gn, axis=-1, keepdims=True)
        - unit * jnp.mean(gn * unit, axis=-1, keepdims=True))).astype(BF16)
    halo_out(1, rows_s)

    acc_s[...] = jnp.zeros_like(acc_s)
    low_of = lax.broadcasted_iota(jnp.int32, (256, 128), 0)

    def pairs(r, carry):
        entry = idx_s[pl.ds(pl.multiple_of(r * 8, 8), 8), :]
        low = jnp.bitwise_and(entry, 255)
        high = jnp.right_shift(entry, 8)
        lefts = []
        rights = []
        for s in range(8):
            value = gs_s[r * 8 + s]
            lefts.append(jnp.concatenate(
                [jnp.where(high[s:s + 1, :] == k, value, 0.0).astype(BF16) for k in range(13)], 0))
            rights.append(jnp.where(low[s:s + 1, :] == low_of, 1.0, 0.0).astype(BF16))
        acc_s[...] += dot_nt(jnp.concatenate(lefts, 1), jnp.concatenate(rights, 1))
        return carry

    lax.fori_loop(0, 21, pairs, 0)
    tpart[...] = jnp.zeros_like(tpart)
    for o in range(13):
        tpart[24 * o:24 * o + 12, :] = acc_s[16 * o:16 * o + 12, 0:128]
        tpart[24 * o + 12:24 * o + 24, :] = acc_s[16 * o:16 * o + 12, 128:256]
    table = [push(tpart.at[pl.ds(pl.multiple_of(24 * step(owner, d, 16), 24), 24)],
                  trecv.at[d - 1], t_ss.at[d - 1], t_rs.at[d - 1], owners[d - 1])
             for d in range(1, 16)]

    total = g_s[lev, lat_rows[-1], :] + gcore[lat_rows[-1], :].astype(F32)
    for n in range(nlat - 1):
        over_lat[n].wait()
        total = total + lat_recv[n].astype(F32)
    turn[...] = jnp.zeros_like(turn)
    turn[0:48, :] = total
    turn[64:112, :] = total
    turned[...] = turn[...].T
    first = lax.broadcasted_iota(jnp.int32, (24, 128), 1) < 64
    for to in range(8):
        for p in range(nz // 2):
            a, b = 16 * p + to, 16 * p + 8 + to
            ypart[to, 24 * p:24 * p + 18, :] = jnp.where(
                first[0:18], turned[18 * a:18 * a + 18, :], turned[18 * b:18 * b + 18, :])
            ypart[to, 24 * p + 18:24 * p + 24, :] = jnp.where(
                first[0:6], turned[576 + 6 * a:576 + 6 * a + 6, :], turned[576 + 6 * b:576 + 6 * b + 6, :])
    ysend[...] = ypart[...].astype(BF16)
    over_y = [push(ysend.at[step(y, d, 8)], yrecv.at[d - 1], y_ss.at[d - 1], y_rs.at[d - 1], y_peers[d - 1])
              for d in range(1, 8)]

    own_block = pl.ds(pl.multiple_of(24 * owner, 24), 24)
    part = tpart[own_block, :]
    for n in range(15):
        table[n].wait()
        part = part + trecv[n]
    tsum[0] = part
    over_z = [push(tsum.at[0], tzrecv.at[n], tz_ss.at[n], tz_rs.at[n], z_peers[n]) for n in range(nz - 1)]

    total = ypart[y]
    for n in range(7):
        over_y[n].wait()
        total = total + yrecv[n].astype(F32)
    zpart[...] = total
    last = [push(zpart.at[pl.ds(pl.multiple_of(24 * (step(z, d, nz) // 2), 24), 24)],
                 zrecv.at[d - 1], z_ss.at[d - 1], z_rs.at[d - 1], z_peers[d - 1])
            for d in range(1, nz)]

    for n in range(nz - 1):
        over_z[n].wait()
        part = part + tzrecv[n]
    tsum[1] = part
    gathered = [push(tsum.at[1], tfull.at[own_block], tg_ss.at[n], tg_rs.at[n], owners[n])
                for n in range(15)]

    loads["own_t"].wait()
    loads["take_t"].wait()
    for f, (base, ref, out) in enumerate(((x_ref, branch_s, xo_ref), (c_ref, rows_s, co_ref))):
        for copy in halo[3 * f:3 * f + 3]:
            copy.wait()
        rolled = dot(own_t_ref[...], ref[...]) + dot(take_t_ref[...], recv[f])
        out[...] = (base[...].astype(F32) + rolled).astype(BF16)

    total = zpart[pl.ds(pl.multiple_of(24 * (z // 2), 24), 24), :]
    for n in range(nz - 1):
        last[n].wait()
        total = total + zrecv[n]
    total = jnp.where(lax.rem(z, 2) == 0, total[:, 0:48], total[:, 64:112]) * norm
    gq_ref[...] = total[0:18]
    gp_ref[...] = total[18:24]

    tfull[own_block, :] = part
    for n in range(15):
        gathered[n].wait()
    for o in range(13):
        width = min(128, POS - 256 * o - 128)
        for h in range(HEADS):
            to_ref[h, :, 256 * o:256 * o + 128] = tfull[24 * o + h:24 * o + h + 1, :]
            to_ref[h, :, 256 * o + 128:256 * o + 128 + width] = tfull[24 * o + 12 + h:24 * o + 13 + h, 0:width]


def block(nlat, nlon, norm, *operands):
    nz = nlon // 8
    sem = pltpu.SemaphoreType.DMA
    vmem = pltpu.VMEM
    loaded = [operands[n] for n in range(13)]
    return pl.pallas_call(
        functools.partial(block_kernel, nlat, nlon, norm),
        in_specs=[pl.BlockSpec(memory_space=pl.ANY)] * 13,
        out_shape=[
            jax.ShapeDtypeStruct((288, 384), BF16),
            jax.ShapeDtypeStruct((288, 384), BF16),
            jax.ShapeDtypeStruct((18, 48), F32),
            jax.ShapeDtypeStruct((6, 48), F32),
            jax.ShapeDtypeStruct((HEADS, 1, POS), F32),
        ],
        scratch_shapes=[vmem(a.shape, a.dtype) for a in loaded] + [
            vmem((288, 384), BF16),
            vmem((288, 384), BF16),
            vmem((168, 128), jnp.int32),
            vmem((12, 24, 128), F32),
            vmem((12, 144, 144), F32),
            vmem((2, 144, 1152), BF16),
            vmem((2, 1152, 144), BF16),
            vmem((288, 384), BF16),
            vmem((2, 384, 144), BF16),
            vmem((2, 384, 144), BF16),
            vmem((2, 384, 144), BF16),
            vmem((288, 1152), BF16),
            vmem((288, 384), F32),
            vmem((288, 128), F32),
            vmem((2, 384, 144), BF16),
            vmem((168, 16, 128), F32),
            vmem((208, 256), F32),
            vmem((288, 384), BF16),
            vmem((288, 384), BF16),
            vmem((2, 384, 768), F32),
            vmem((384, 128), F32),
            vmem((2, 208, 384), BF16),
            vmem((2, 208, 384), BF16),
            vmem((2, 208, 384), BF16),
            vmem((2, 208, 384), BF16),
            vmem((384, 768), BF16),
            vmem((384, 768), BF16),
            vmem((nlat - 1, 48, 768), BF16),
            vmem((nlat - 1, 48, 768), BF16),
            vmem((128, 768), F32),
            vmem((768, 128), F32),
            vmem((8, 48, 128), F32),
            vmem((8, 48, 128), BF16),
            vmem((7, 48, 128), BF16),
            vmem((48, 128), F32),
            vmem((nz - 1, 24, 128), F32),
            vmem((15, 24, 128), F32),
            vmem((2, 24, 128), F32),
            vmem((nz - 1, 24, 128), F32),
            vmem((384, 128), F32),
            sem((13,)), sem((6,)), sem((6,)), sem((6,)), sem((6,)), sem((nlat,)), sem((nlat,)),
            sem((nlat - 1,)), sem((nlat - 1,)),
            sem((7,)), sem((7,)), sem((nz - 1,)), sem((nz - 1,)),
            sem((15,)), sem((15,)), sem((nz - 1,)), sem((nz - 1,)), sem((15,)), sem((15,)),
        ],
        compiler_params=pltpu.CompilerParams(
            collective_id=0, has_side_effects=True, vmem_limit_bytes=56 * 1024 * 1024),
        name="block",
    )(*operands)


def publish_kernel(*refs):
    sems = refs[-1]
    copies = [pltpu.make_async_copy(refs[n], refs[5 + n], sems.at[n]) for n in range(5)]
    for copy in copies:
        copy.start()
    for copy in copies:
        copy.wait()


def publish(*results):
    return pl.pallas_call(
        publish_kernel,
        in_specs=[pl.BlockSpec(memory_space=pl.ANY)] * 5,
        out_specs=[pl.BlockSpec(memory_space=pl.ANY)] * 5,
        out_shape=[jax.ShapeDtypeStruct(r.shape, r.dtype) for r in results],
        scratch_shapes=[pltpu.SemaphoreType.DMA((5,))],
        name="publish",
    )(*results)


def body(tokens, cotangent, w_qkv, w_proj, bias_table, bias_index, region_ids):
    levels, rows, columns, width = tokens.shape
    nlev, nlat, nlon = lax.axis_size("lev"), lax.axis_size("lat"), lax.axis_size("lon")
    norm = 1.0 / math.sqrt(levels * nlev * rows * nlat * columns * nlon)
    send, own, recv = permutations()
    send, own, recv, send_t, own_t, recv_t = [
        jnp.asarray(m, BF16) for m in (send, own, recv, send.T, own.T, recv.T)]
    results = block(
        nlat, nlon, norm, tokens.reshape(288, width), cotangent.reshape(288, width), w_qkv, w_proj,
        bias_table.transpose(1, 0, 2), bias_index[0], region_ids, send, own, recv, send_t, own_t, recv_t)
    block_out, grad_tokens, gq, gp, table = publish(*results)
    return (block_out.reshape(tokens.shape), grad_tokens.reshape(tokens.shape), gq.T, gp.T,
            table.transpose(1, 0, 2))


def solution(mesh):
    return jax.shard_map(
        body,
        mesh=mesh,
        in_specs=(
            jax.P("lev", "lat", "lon", None),
            jax.P("lev", "lat", "lon", None),
            jax.P(),
            jax.P(),
            jax.P("lat", None, None),
            jax.P("lat", None, None),
            jax.P("lat", "lon"),
        ),
        out_specs=(
            jax.P("lev", "lat", "lon", None),
            jax.P("lev", "lat", "lon", None),
            jax.P("lat", ("lev", "lon")),
            jax.P("lat", ("lev", "lon")),
            jax.P("lat", None, None),
        ),
        check_vma=False,
    )
```

```python
import functools
import math

import jax
import jax.numpy as jnp
import numpy as np
from jax import lax
from jax.experimental import pallas as pl
from jax.experimental.pallas import tpu as pltpu

F32 = jnp.float32
BF16 = jnp.bfloat16
HEADS = 12
WIN = 144
WIDTH = 384
POS = 3312
GRAIN = 32767 / 5
FACTOR = 32 ** (-0.5)


def dot(a, b):
    return lax.dot_general(a, b, (((1,), (0,)), ((), ())), preferred_element_type=F32)


def dot_nt(a, b):
    return lax.dot_general(a, b, (((1,), (1,)), ((), ())), preferred_element_type=F32)


def pack_tail(block):
    rows = []
    for q in range(3):
        parts = []
        for b in range(8):
            at = 64 * q + 8 * b
            if at < WIN:
                parts.append(block[at:at + 8, :])
            else:
                parts.append(jnp.full((8, 16), -1, block.dtype))
        rows.append(jnp.concatenate(parts, 1))
    return jnp.concatenate(rows, 0)


PIECES = ((0, 112), (112, 48), (160, 48))
MESH = pl.DeviceIdType.MESH


@functools.lru_cache(None)
def permutations():
    place = {}
    for l in range(2):
        for r in range(3):
            for c in range(6, 24):
                place[l, r, c] = l * 54 + r * 18 + c - 6
        for r in range(3, 6):
            for c in range(6):
                place[l, r, c] = 112 + l * 18 + (r - 3) * 6 + c
        for r in range(3):
            for c in range(6):
                place[l, r, c] = 160 + l * 18 + r * 6 + c
    send = np.zeros((208, 288), np.float32)
    for (l, r, c), at in place.items():
        send[at, l * 144 + r * 24 + c] = 1
    own = np.zeros((288, 288), np.float32)
    recv = np.zeros((288, 208), np.float32)
    for w in range(2):
        for l in range(2):
            for r in range(6):
                for c in range(12):
                    row = w * 144 + l * 72 + r * 12 + c
                    at, col = r + 3, 12 * w + c + 6
                    if at < 6 and col < 24:
                        own[row, l * 144 + at * 24 + col] = 1
                    else:
                        recv[row, place[l, at % 6, col % 24]] = 1
    return send, own, recv


def step(index, by, count):
    return lax.rem(index + (by + count), count)


def block_kernel(nlat, nlon, norm, x_hbm, c_hbm, wq_hbm, wp_hbm, tab_hbm, idx_hbm, reg_hbm,
                 take_hbm, own_hbm, put_hbm, take_t_hbm, own_t_hbm, put_t_hbm,
                 xo_ref, co_ref, gq_ref, gp_ref, to_ref,
                 x_ref, c_ref, wq_ref, wp_ref, tab_ref, idx_ref, reg_ref,
                 take_ref, own_ref, put_ref, take_t_ref, own_t_ref, put_t_ref,
                 xw_s, cw_s, words_s, rows_of_table, idx_s, tail_s, bias_s, qkv_s, qkvt_s, gm_s, gmt_s, mixt_s, gqt_s, gp_s,
                 unit_s, inv_s, normt_s, gs_s, acc_s, branch_s, rows_s, g_s, tpart,
                 send_in, recv_in, send, recv, gsend, gcore, lat_send, lat_recv, turn, turned, ypart, ysend, yrecv,
                 zpart, zrecv, trecv, tsum, tzrecv, tfull,
                 load_sem, in_ss, in_rs, halo_ss, halo_rs, core_ss, core_rs, lat_ss, lat_rs,
                 y_ss, y_rs, z_ss, z_rs, t_ss, t_rs, tz_ss, tz_rs, tg_ss, tg_rs):
    names = ("x", "c", "take", "own", "put", "tab", "idx", "reg", "wq", "wp", "own_t", "take_t", "put_t")
    from_to = ((x_hbm, x_ref), (c_hbm, c_ref), (take_hbm, take_ref), (own_hbm, own_ref), (put_hbm, put_ref),
                (tab_hbm, tab_ref), (idx_hbm, idx_ref), (reg_hbm, reg_ref), (wq_hbm, wq_ref), (wp_hbm, wp_ref),
                (own_t_hbm, own_t_ref), (take_t_hbm, take_t_ref), (put_t_hbm, put_t_ref))
    loads = {}
    for n, (name, (src, dst)) in enumerate(zip(names, from_to)):
        loads[name] = pltpu.make_async_copy(src, dst, load_sem.at[n])
        loads[name].start()

    nz = nlon // 8
    lev, lat, lon = lax.axis_index("lev"), lax.axis_index("lat"), lax.axis_index("lon")
    z, y = lon // 8, lax.rem(lon, 8)
    owner = lev * 8 + y

    def at_owner(o):
        return {"lev": o // 8, "lat": lat, "lon": z * 8 + lax.rem(o, 8)}

    core_peer = {"lev": 1 - lev, "lat": lat, "lon": lon}
    lat_peers = [{"lev": lev, "lat": step(lat, d, nlat), "lon": lon} for d in range(1, nlat)]
    y_peers = [{"lev": lev, "lat": lat, "lon": z * 8 + step(y, d, 8)} for d in range(1, 8)]
    z_peers = [{"lev": lev, "lat": lat, "lon": step(z, d, nz) * 8 + y} for d in range(1, nz)]
    owners = [at_owner(step(owner, d, 16)) for d in range(1, 16)]
    after, before = [
        [{"lev": lev, "lat": step(lat, by, nlat), "lon": lon},
         {"lev": lev, "lat": lat, "lon": step(lon, by, nlon)},
         {"lev": lev, "lat": step(lat, by, nlat), "lon": step(lon, by, nlon)}] for by in (1, -1)]
    barrier = pltpu.get_barrier_semaphore()
    greet = after[1:] + before[1:] + lat_peers + owners + z_peers
    for device in greet:
        pl.semaphore_signal(barrier, inc=1, device_id=device, device_id_type=MESH)

    def push(src, dst, ss, rs, device):
        copy = pltpu.make_async_remote_copy(
            src_ref=src, dst_ref=dst, send_sem=ss, recv_sem=rs, device_id=device, device_id_type=MESH)
        copy.start()
        return copy

    for name in ("x", "c", "take"):
        loads[name].wait()
    for f, ref in enumerate((x_ref, c_ref)):
        send_in[f] = dot(take_ref[...], ref[...]).astype(BF16)
    pl.semaphore_wait(barrier, len(greet))
    arrive = [push(send_in.at[f, pl.ds(at, size)], recv_in.at[f, pl.ds(at, size)],
                   in_ss.at[3 * f + n], in_rs.at[3 * f + n], before[n])
              for f in range(2) for n, (at, size) in enumerate(PIECES)]

    for name in ("tab", "idx"):
        loads[name].wait()
    words_s[...] = jnp.zeros_like(words_s)
    for h in range(HEADS):
        rows_of_table[h:h + 1, :] = tab_ref[h]
    upper = jnp.floor(rows_of_table[0:6, :] * GRAIN + 0.5).astype(jnp.int32)
    lower = jnp.floor(rows_of_table[6:12, :] * GRAIN + 0.5).astype(jnp.int32)
    words_s[0:6, 0:POS] = jnp.left_shift(upper, 16) + jnp.bitwise_and(lower, 65535)
    index_t = idx_ref[...].T
    idx_s[0:WIN, :] = index_t[:, 0:128]
    idx_s[WIN:168, :] = pack_tail(index_t[:, 128:144])

    def look_up(r, store):
        at = pl.multiple_of(r * 8, 8)
        entry = idx_s[pl.ds(at, 8), :]
        low = jnp.bitwise_and(entry, 127)
        high = jnp.right_shift(entry, 7)
        found = [jnp.zeros((8, 128), jnp.int32) for _ in range(6)]
        for k in range(26):
            here = high == k
            for h in range(6):
                line = jnp.broadcast_to(words_s[h:h + 1, 128 * k:128 * k + 128], (8, 128))
                got = jnp.take_along_axis(line, low, axis=1, mode="promise_in_bounds")
                found[h] = jnp.where(here, got, found[h])
        for h in range(6):
            store(h, at, jnp.right_shift(found[h], 16).astype(F32) * (1 / GRAIN))
            half = jnp.right_shift(jnp.left_shift(found[h], 16), 16)
            store(h + 6, at, half.astype(F32) * (1 / GRAIN))

    def main_rows(r, carry):
        def store(h, at, value):
            bias_s[h, pl.ds(at, 8), 0:128] = value
        look_up(r, store)
        return carry

    def tail_rows(r, carry):
        def store(h, at, value):
            tail_s[h, pl.ds(pl.multiple_of(at - WIN, 8), 8), :] = value
        look_up(r, store)
        return carry

    lax.fori_loop(0, 18, main_rows, 0)
    lax.fori_loop(18, 21, tail_rows, 0)

    def spread(h, carry):
        for at in range(0, WIN, 8):
            q, b = at // 64, at % 64 // 8
            bias_s[h, at:at + 8, 128:144] = tail_s[h, 8 * q:8 * q + 8, 16 * b:16 * b + 16]
        return carry

    lax.fori_loop(0, HEADS, spread, 0)
    gs_s[...] = jnp.zeros_like(gs_s)

    loads["reg"].wait()
    region = reg_ref[...].astype(F32).astype(BF16)
    col_of = lax.broadcasted_iota(jnp.int32, (24, WIN), 0)
    place = lax.broadcasted_iota(jnp.int32, (24, WIN), 1)
    row_of = lax.broadcasted_iota(jnp.int32, (6, WIN), 0)
    row_at = lax.rem(lax.broadcasted_iota(jnp.int32, (6, WIN), 1), 72) // 12
    allowed = []
    for w in range(2):
        choose = jnp.where(col_of == lax.rem(place, 12) + 12 * w, 1.0, 0.0).astype(BF16)
        line = jnp.sum(jnp.where(row_of == row_at, dot(region, choose), 0.0), axis=0, keepdims=True)
        down = jnp.broadcast_to(line, (128, WIN)).T
        allowed.append(down[:, 0:1] == line)

    loads["own"].wait()
    loads["put"].wait()
    mine = [dot(own_ref[...], ref[...]) for ref in (x_ref, c_ref)]

    def assemble(f, ref):
        for copy in arrive[3 * f:3 * f + 3]:
            copy.wait()
        ref[...] = (mine[f] + dot(put_ref[...], recv_in[f])).astype(BF16)

    assemble(0, xw_s)

    loads["wq"].wait()
    loads["wp"].wait()
    flat = xw_s[...].astype(F32)
    center = flat - jnp.mean(flat, axis=-1, keepdims=True)
    inverse = lax.rsqrt(jnp.mean(center * center, axis=-1, keepdims=True) + 1e-05)
    unit = center * inverse
    unit_s[...] = unit
    inv_s[...] = jnp.broadcast_to(inverse, inv_s.shape)
    normed = unit.astype(BF16)
    packed = dot(normed, wq_ref[...]).astype(BF16)
    for w in range(2):
        at = slice(WIN * w, WIN * w + WIN)
        qkv_s[w] = packed[at]
        qkvt_s[w] = packed[at].T
        normt_s[w] = normed[at].T
    assemble(1, cw_s)
    cot = cw_s[...]
    gm_s[...] = dot_nt(cot, wp_ref[...]).astype(BF16)
    for w in range(2):
        at = slice(WIN * w, WIN * w + WIN)
        gmt_s[w] = dot_nt(wp_ref[...], cot[at]).astype(BF16)

    lane = lax.broadcasted_iota(jnp.int32, (WIN, 128), 1)
    line_of = lax.broadcasted_iota(jnp.int32, (128, WIN), 0)

    def group(g, carry):
        off = pl.multiple_of(g * 128, 128)
        grad_key = [None, None]
        grad_value = [None, None]
        for a in range(4):
            h = g * 4 + a
            own_line = (line_of >= 32 * a) & (line_of < 32 * a + 32)
            own_lane = (lane >= 32 * a) & (lane < 32 * a + 32)
            total = None
            bias = bias_s[h]
            for w in range(2):
                q = qkv_s[w, :, pl.ds(off, 128)]
                k = qkv_s[w, :, pl.ds(off + 384, 128)]
                v = qkv_s[w, :, pl.ds(off + 768, 128)]
                qt = qkvt_s[w, pl.ds(off, 128), :]
                gmt = gmt_s[w, pl.ds(off, 128), :]
                here = pl.multiple_of(off + 32 * a, 32)
                kt = qkvt_s[w, pl.ds(384 + here, 32), :]
                vt = qkvt_s[w, pl.ds(768 + here, 32), :]
                gm = gm_s[pl.ds(WIN * w, WIN), pl.ds(off, 128)]
                zero = jnp.zeros((), BF16)
                s = dot(k, jnp.where(own_line, qt, zero)) * FACTOR + bias
                s = jnp.where(allowed[w], s, -1e30)
                e = jnp.exp(s - jnp.max(s, axis=0, keepdims=True))
                p = e * (1.0 / jnp.sum(e, axis=0, keepdims=True))
                pb = p.astype(BF16)
                mixt_s[w, pl.ds(here, 32), :] = dot(vt, pb).astype(BF16)
                gpr = dot(v, jnp.where(own_line, gmt, zero))
                gv = dot(pb, gm)
                gs = p * (gpr - jnp.sum(p * gpr, axis=0, keepdims=True))
                sc = (gs * FACTOR).astype(BF16)
                gqt_s[w, pl.ds(here, 32), :] = dot(kt, sc).astype(BF16)
                gk = dot(sc, q)
                grad_key[w] = gk if a == 0 else jnp.where(own_lane, gk, grad_key[w])
                grad_value[w] = gv if a == 0 else jnp.where(own_lane, gv, grad_value[w])
                total = gs if w == 0 else total + gs
            gs_s[0:WIN, pl.ds(h, 1), :] = total[:, 0:128].reshape(WIN, 1, 128)
            gs_s[WIN:168, pl.ds(h, 1), :] = pack_tail(total[:, 128:144]).reshape(24, 1, 128)
        for w in range(2):
            rows = slice(WIN * w, WIN * w + WIN)
            gp_s[rows, pl.ds(off + 384, 128)] = grad_key[w].astype(BF16)
            gp_s[rows, pl.ds(off + 768, 128)] = grad_value[w].astype(BF16)
        return carry

    lax.fori_loop(0, 3, group, 0, unroll=True)

    for w in range(2):
        gp_s[WIN * w:WIN * w + WIN, 0:384] = gqt_s[w].T
    for half in range(2):
        part = [dot(normt_s[w], gp_s[WIN * w:WIN * w + WIN, 576 * half:576 * half + 576]) for w in range(2)]
        g_s[half, :, 0:576] = part[0] + part[1]
        part = [dot(mixt_s[w], cw_s[WIN * w:WIN * w + WIN, 192 * half:192 * half + 192]) for w in range(2)]
        g_s[half, :, 576:768] = part[0] + part[1]
    gsend[...] = g_s[1 - lev].astype(BF16)
    lat_rows = [pl.ds(pl.multiple_of(48 * step(lat, d, nlat), 48), 48) for d in range(1, nlat + 1)]
    core = [push(gsend.at[rows], gcore.at[rows], core_ss.at[n], core_rs.at[n], core_peer)
            for n, rows in enumerate(lat_rows)]

    loads["put_t"].wait()
    halo = []

    def halo_out(f, ref):
        send[f] = dot(put_t_ref[...], ref[...]).astype(BF16)
        for n, (at, size) in enumerate(PIECES):
            halo.append(push(send.at[f, pl.ds(at, size)], recv.at[f, pl.ds(at, size)],
                             halo_ss.at[3 * f + n], halo_rs.at[3 * f + n], after[n]))

    for w in range(2):
        branch_s[WIN * w:WIN * w + WIN, :] = dot(mixt_s[w].T, wp_ref[...]).astype(BF16)

    over_lat = []
    for n in range(nlat - 1):
        core[n].wait()
        lat_send[n] = (g_s[lev, lat_rows[n], :] + gcore[lat_rows[n], :].astype(F32)).astype(BF16)
        over_lat.append(push(lat_send.at[n], lat_recv.at[n], lat_ss.at[n], lat_rs.at[n], lat_peers[n]))
    core[nlat - 1].wait()
    halo_out(0, branch_s)

    gn = dot_nt(gp_s[...], wq_ref[...])
    unit = unit_s[...]
    rows_s[...] = (inv_s[:, 0:1] * (
        gn - jnp.mean(gn, axis=-1, keepdims=True)
        - unit * jnp.mean(gn * unit, axis=-1, keepdims=True))).astype(BF16)
    halo_out(1, rows_s)

    acc_s[...] = jnp.zeros_like(acc_s)
    low_of = lax.broadcasted_iota(jnp.int32, (256, 128), 0)

    def pairs(r, carry):
        entry = idx_s[pl.ds(pl.multiple_of(r * 8, 8), 8), :]
        low = jnp.bitwise_and(entry, 255)
        high = jnp.right_shift(entry, 8)
        lefts = []
        rights = []
        for s in range(8):
            value = gs_s[r * 8 + s]
            lefts.append(jnp.concatenate(
                [jnp.where(high[s:s + 1, :] == k, value, 0.0).astype(BF16) for k in range(13)], 0))
            rights.append(jnp.where(low[s:s + 1, :] == low_of, 1.0, 0.0).astype(BF16))
        acc_s[...] += dot_nt(jnp.concatenate(lefts, 1), jnp.concatenate(rights, 1))
        return carry

    lax.fori_loop(0, 21, pairs, 0, unroll=3)
    tpart[...] = jnp.zeros_like(tpart)
    for o in range(13):
        tpart[24 * o:24 * o + 12, :] = acc_s[16 * o:16 * o + 12, 0:128]
        tpart[24 * o + 12:24 * o + 24, :] = acc_s[16 * o:16 * o + 12, 128:256]
    table = [push(tpart.at[pl.ds(pl.multiple_of(24 * step(owner, d, 16), 24), 24)],
                  trecv.at[d - 1], t_ss.at[d - 1], t_rs.at[d - 1], owners[d - 1])
             for d in range(1, 16)]

    total = g_s[lev, lat_rows[-1], :] + gcore[lat_rows[-1], :].astype(F32)
    for n in range(nlat - 1):
        over_lat[n].wait()
        total = total + lat_recv[n].astype(F32)
    turn[...] = jnp.zeros_like(turn)
    turn[0:48, :] = total
    turn[64:112, :] = total
    turned[...] = turn[...].T
    first = lax.broadcasted_iota(jnp.int32, (24, 128), 1) < 64
    for to in range(8):
        for p in range(nz // 2):
            a, b = 16 * p + to, 16 * p + 8 + to
            ypart[to, 24 * p:24 * p + 18, :] = jnp.where(
                first[0:18], turned[18 * a:18 * a + 18, :], turned[18 * b:18 * b + 18, :])
            ypart[to, 24 * p + 18:24 * p + 24, :] = jnp.where(
                first[0:6], turned[576 + 6 * a:576 + 6 * a + 6, :], turned[576 + 6 * b:576 + 6 * b + 6, :])
    ysend[...] = ypart[...].astype(BF16)
    over_y = [push(ysend.at[step(y, d, 8)], yrecv.at[d - 1], y_ss.at[d - 1], y_rs.at[d - 1], y_peers[d - 1])
              for d in range(1, 8)]

    own_block = pl.ds(pl.multiple_of(24 * owner, 24), 24)
    part = tpart[own_block, :]
    for n in range(15):
        table[n].wait()
        part = part + trecv[n]
    tsum[0] = part
    over_z = [push(tsum.at[0], tzrecv.at[n], tz_ss.at[n], tz_rs.at[n], z_peers[n]) for n in range(nz - 1)]

    total = ypart[y]
    for n in range(7):
        over_y[n].wait()
        total = total + yrecv[n].astype(F32)
    zpart[...] = total
    last = [push(zpart.at[pl.ds(pl.multiple_of(24 * (step(z, d, nz) // 2), 24), 24)],
                 zrecv.at[d - 1], z_ss.at[d - 1], z_rs.at[d - 1], z_peers[d - 1])
            for d in range(1, nz)]

    for n in range(nz - 1):
        over_z[n].wait()
        part = part + tzrecv[n]
    tsum[1] = part
    gathered = [push(tsum.at[1], tfull.at[own_block], tg_ss.at[n], tg_rs.at[n], owners[n])
                for n in range(15)]

    loads["own_t"].wait()
    loads["take_t"].wait()
    for f, (base, ref, out) in enumerate(((x_ref, branch_s, xo_ref), (c_ref, rows_s, co_ref))):
        for copy in halo[3 * f:3 * f + 3]:
            copy.wait()
        rolled = dot(own_t_ref[...], ref[...]) + dot(take_t_ref[...], recv[f])
        out[...] = (base[...].astype(F32) + rolled).astype(BF16)

    total = zpart[pl.ds(pl.multiple_of(24 * (z // 2), 24), 24), :]
    for n in range(nz - 1):
        last[n].wait()
        total = total + zrecv[n]
    total = jnp.where(lax.rem(z, 2) == 0, total[:, 0:48], total[:, 64:112]) * norm
    gq_ref[...] = total[0:18]
    gp_ref[...] = total[18:24]

    tfull[own_block, :] = part
    for n in range(15):
        gathered[n].wait()
    for o in range(13):
        width = min(128, POS - 256 * o - 128)
        for h in range(HEADS):
            to_ref[h, :, 256 * o:256 * o + 128] = tfull[24 * o + h:24 * o + h + 1, :]
            to_ref[h, :, 256 * o + 128:256 * o + 128 + width] = tfull[24 * o + 12 + h:24 * o + 13 + h, 0:width]


def block(nlat, nlon, norm, *operands):
    nz = nlon // 8
    sem = pltpu.SemaphoreType.DMA
    vmem = pltpu.VMEM
    loaded = [operands[n] for n in range(13)]
    return pl.pallas_call(
        functools.partial(block_kernel, nlat, nlon, norm),
        in_specs=[pl.BlockSpec(memory_space=pl.ANY)] * 13,
        out_shape=[
            jax.ShapeDtypeStruct((288, 384), BF16),
            jax.ShapeDtypeStruct((288, 384), BF16),
            jax.ShapeDtypeStruct((18, 48), F32),
            jax.ShapeDtypeStruct((6, 48), F32),
            jax.ShapeDtypeStruct((HEADS, 1, POS), F32),
        ],
        scratch_shapes=[vmem(a.shape, a.dtype) for a in loaded] + [
            vmem((288, 384), BF16),
            vmem((288, 384), BF16),
            vmem((8, 3328), jnp.int32),
            vmem((16, POS), F32),
            vmem((168, 128), jnp.int32),
            vmem((12, 24, 128), F32),
            vmem((12, 144, 144), F32),
            vmem((2, 144, 1152), BF16),
            vmem((2, 1152, 144), BF16),
            vmem((288, 384), BF16),
            vmem((2, 384, 144), BF16),
            vmem((2, 384, 144), BF16),
            vmem((2, 384, 144), BF16),
            vmem((288, 1152), BF16),
            vmem((288, 384), F32),
            vmem((288, 128), F32),
            vmem((2, 384, 144), BF16),
            vmem((168, 16, 128), F32),
            vmem((208, 256), F32),
            vmem((288, 384), BF16),
            vmem((288, 384), BF16),
            vmem((2, 384, 768), F32),
            vmem((384, 128), F32),
            vmem((2, 208, 384), BF16),
            vmem((2, 208, 384), BF16),
            vmem((2, 208, 384), BF16),
            vmem((2, 208, 384), BF16),
            vmem((384, 768), BF16),
            vmem((384, 768), BF16),
            vmem((nlat - 1, 48, 768), BF16),
            vmem((nlat - 1, 48, 768), BF16),
            vmem((128, 768), F32),
            vmem((768, 128), F32),
            vmem((8, 48, 128), F32),
            vmem((8, 48, 128), BF16),
            vmem((7, 48, 128), BF16),
            vmem((48, 128), F32),
            vmem((nz - 1, 24, 128), F32),
            vmem((15, 24, 128), F32),
            vmem((2, 24, 128), F32),
            vmem((nz - 1, 24, 128), F32),
            vmem((384, 128), F32),
            sem((13,)), sem((6,)), sem((6,)), sem((6,)), sem((6,)), sem((nlat,)), sem((nlat,)),
            sem((nlat - 1,)), sem((nlat - 1,)),
            sem((7,)), sem((7,)), sem((nz - 1,)), sem((nz - 1,)),
            sem((15,)), sem((15,)), sem((nz - 1,)), sem((nz - 1,)), sem((15,)), sem((15,)),
        ],
        compiler_params=pltpu.CompilerParams(
            collective_id=0, has_side_effects=True, vmem_limit_bytes=56 * 1024 * 1024),
        name="block",
    )(*operands)


def publish_kernel(*refs):
    results, outs, held = refs[0:5], refs[5:10], refs[10:15]
    in_sem, out_sem = refs[15:]
    loads = [pltpu.make_async_copy(results[n], held[n], in_sem.at[n]) for n in range(5)]
    stores = [pltpu.make_async_copy(held[n], outs[n], out_sem.at[n]) for n in range(5)]
    for copy in loads:
        copy.start()
    for n in range(5):
        loads[n].wait()
        stores[n].start()
    for copy in stores:
        copy.wait()


def publish(*results):
    sem = pltpu.SemaphoreType.DMA
    return pl.pallas_call(
        publish_kernel,
        in_specs=[pl.BlockSpec(memory_space=pl.ANY)] * 5,
        out_specs=[pl.BlockSpec(memory_space=pl.ANY)] * 5,
        out_shape=[jax.ShapeDtypeStruct(r.shape, r.dtype) for r in results],
        scratch_shapes=[pltpu.VMEM(r.shape, r.dtype) for r in results] + [sem((5,)), sem((5,))],
        compiler_params=pltpu.CompilerParams(vmem_limit_bytes=56 * 1024 * 1024),
        name="publish",
    )(*results)


def body(tokens, cotangent, w_qkv, w_proj, bias_table, bias_index, region_ids):
    levels, rows, columns, width = tokens.shape
    nlev, nlat, nlon = lax.axis_size("lev"), lax.axis_size("lat"), lax.axis_size("lon")
    norm = 1.0 / math.sqrt(levels * nlev * rows * nlat * columns * nlon)
    send, own, recv = permutations()
    send, own, recv, send_t, own_t, recv_t = [
        jnp.asarray(m, BF16) for m in (send, own, recv, send.T, own.T, recv.T)]
    results = block(
        nlat, nlon, norm, tokens.reshape(288, width), cotangent.reshape(288, width), w_qkv, w_proj,
        bias_table.transpose(1, 0, 2), bias_index[0], region_ids, send, own, recv, send_t, own_t, recv_t)
    block_out, grad_tokens, gq, gp, table = publish(*results)
    return (block_out.reshape(tokens.shape), grad_tokens.reshape(tokens.shape), gq.T, gp.T,
            table.transpose(1, 0, 2))


def solution(mesh):
    return jax.shard_map(
        body,
        mesh=mesh,
        in_specs=(
            jax.P("lev", "lat", "lon", None),
            jax.P("lev", "lat", "lon", None),
            jax.P(),
            jax.P(),
            jax.P("lat", None, None),
            jax.P("lat", None, None),
            jax.P("lat", "lon"),
        ),
        out_specs=(
            jax.P("lev", "lat", "lon", None),
            jax.P("lev", "lat", "lon", None),
            jax.P("lat", ("lev", "lon")),
            jax.P("lat", ("lev", "lon")),
            jax.P("lat", None, None),
        ),
        check_vma=False,
    )
```

```python
import functools
import math

import jax
import jax.numpy as jnp
import numpy as np
from jax import lax
from jax.experimental import pallas as pl
from jax.experimental.pallas import tpu as pltpu

F32 = jnp.float32
BF16 = jnp.bfloat16
HEADS = 12
WIN = 144
WIDTH = 384
POS = 3312
GRAIN = 32767 / 5
FACTOR = 32 ** (-0.5)


def dot(a, b):
    return lax.dot_general(a, b, (((1,), (0,)), ((), ())), preferred_element_type=F32)


def dot_nt(a, b):
    return lax.dot_general(a, b, (((1,), (1,)), ((), ())), preferred_element_type=F32)


def pack_tail(block):
    rows = []
    for q in range(3):
        parts = []
        for b in range(8):
            at = 64 * q + 8 * b
            if at < WIN:
                parts.append(block[at:at + 8, :])
            else:
                parts.append(jnp.full((8, 16), -1, block.dtype))
        rows.append(jnp.concatenate(parts, 1))
    return jnp.concatenate(rows, 0)


PIECES = ((0, 112), (112, 48), (160, 48))
MESH = pl.DeviceIdType.MESH


@functools.lru_cache(None)
def permutations():
    place = {}
    for l in range(2):
        for r in range(3):
            for c in range(6, 24):
                place[l, r, c] = l * 54 + r * 18 + c - 6
        for r in range(3, 6):
            for c in range(6):
                place[l, r, c] = 112 + l * 18 + (r - 3) * 6 + c
        for r in range(3):
            for c in range(6):
                place[l, r, c] = 160 + l * 18 + r * 6 + c
    send = np.zeros((208, 288), np.float32)
    for (l, r, c), at in place.items():
        send[at, l * 144 + r * 24 + c] = 1
    own = np.zeros((288, 288), np.float32)
    recv = np.zeros((288, 208), np.float32)
    for w in range(2):
        for l in range(2):
            for r in range(6):
                for c in range(12):
                    row = w * 144 + l * 72 + r * 12 + c
                    at, col = r + 3, 12 * w + c + 6
                    if at < 6 and col < 24:
                        own[row, l * 144 + at * 24 + col] = 1
                    else:
                        recv[row, place[l, at % 6, col % 24]] = 1
    return send, own, recv


def step(index, by, count):
    return lax.rem(index + (by + count), count)


def block_kernel(nlat, nlon, norm, x_hbm, c_hbm, wq_hbm, wp_hbm, tab_hbm, idx_hbm, reg_hbm,
                 take_hbm, own_hbm, put_hbm, take_t_hbm, own_t_hbm, put_t_hbm,
                 xo_ref, co_ref, gq_ref, gp_ref, to_ref,
                 x_ref, c_ref, wq_ref, wp_ref, tab_ref, idx_ref, reg_ref,
                 take_ref, own_ref, put_ref, take_t_ref, own_t_ref, put_t_ref,
                 xw_s, cw_s, words_s, rows_of_table, idx_s, tail_s, bias_s, qkv_s, qkvt_s, gm_s, gmt_s, mixt_s, gqt_s, gp_s,
                 unit_s, inv_s, normt_s, gs_s, acc_s, branch_s, rows_s, g_s, tpart,
                 send_in, recv_in, send, recv, gsend, gcore, lat_send, lat_recv, turn, turned, ypart, ysend, yrecv,
                 zpart, zrecv, gs_send, gs_recv, tsend, trecv, tz, tfull,
                 load_sem, in_ss, in_rs, halo_ss, halo_rs, core_ss, core_rs, lat_ss, lat_rs,
                 y_ss, y_rs, z_ss, z_rs, t_ss, t_rs, tz_ss, tz_rs, tg_ss, tg_rs, gs_ss, gs_rs):
    nz = nlon // 8
    lev, lat, lon = lax.axis_index("lev"), lax.axis_index("lat"), lax.axis_index("lon")
    z, y = lon // 8, lax.rem(lon, 8)
    owner = lev * 8 + y

    def at_owner(o):
        return {"lev": o // 8, "lat": lat, "lon": z * 8 + lax.rem(o, 8)}

    core_peer = {"lev": 1 - lev, "lat": lat, "lon": lon}
    lat_peers = [{"lev": lev, "lat": step(lat, d, nlat), "lon": lon} for d in range(1, nlat)]
    y_peers = [{"lev": lev, "lat": lat, "lon": z * 8 + step(y, d, 8)} for d in range(1, 8)]
    z_peers = [{"lev": lev, "lat": lat, "lon": step(z, d, nz) * 8 + y} for d in range(1, nz)]
    owners = [at_owner(step(owner, d, 16)) for d in range(1, 16)]
    after, before = [
        [{"lev": lev, "lat": step(lat, by, nlat), "lon": lon},
         {"lev": lev, "lat": lat, "lon": step(lon, by, nlon)},
         {"lev": lev, "lat": step(lat, by, nlat), "lon": step(lon, by, nlon)}] for by in (1, -1)]
    barrier = pltpu.get_barrier_semaphore()
    greet = after[1:] + before[1:] + lat_peers + owners + z_peers
    for device in greet:
        pl.semaphore_signal(barrier, inc=1, device_id=device, device_id_type=MESH)

    names = ("x", "c", "take", "own", "put", "tab", "idx", "reg", "wq", "wp", "own_t", "take_t", "put_t")
    from_to = ((x_hbm, x_ref), (c_hbm, c_ref), (take_hbm, take_ref), (own_hbm, own_ref), (put_hbm, put_ref),
                (tab_hbm, tab_ref), (idx_hbm, idx_ref), (reg_hbm, reg_ref), (wq_hbm, wq_ref), (wp_hbm, wp_ref),
                (own_t_hbm, own_t_ref), (take_t_hbm, take_t_ref), (put_t_hbm, put_t_ref))
    loads = {}
    for n, (name, (src, dst)) in enumerate(zip(names, from_to)):
        loads[name] = pltpu.make_async_copy(src, dst, load_sem.at[n])
        loads[name].start()

    def push(src, dst, ss, rs, device):
        copy = pltpu.make_async_remote_copy(
            src_ref=src, dst_ref=dst, send_sem=ss, recv_sem=rs, device_id=device, device_id_type=MESH)
        copy.start()
        return copy

    for name in ("x", "c", "take"):
        loads[name].wait()
    for f, ref in enumerate((x_ref, c_ref)):
        send_in[f] = dot(take_ref[...], ref[...]).astype(BF16)
    pl.semaphore_wait(barrier, len(greet))
    arrive = [push(send_in.at[f, pl.ds(at, size)], recv_in.at[f, pl.ds(at, size)],
                   in_ss.at[3 * f + n], in_rs.at[3 * f + n], before[n])
              for f in range(2) for n, (at, size) in enumerate(PIECES)]

    for name in ("tab", "idx"):
        loads[name].wait()
    words_s[...] = jnp.zeros_like(words_s)
    for h in range(HEADS):
        rows_of_table[h:h + 1, :] = tab_ref[h]
    upper = jnp.floor(rows_of_table[0:6, :] * GRAIN + 0.5).astype(jnp.int32)
    lower = jnp.floor(rows_of_table[6:12, :] * GRAIN + 0.5).astype(jnp.int32)
    words_s[0:6, 0:POS] = jnp.left_shift(upper, 16) + jnp.bitwise_and(lower, 65535)
    index_t = idx_ref[...].T
    idx_s[0:WIN, :] = index_t[:, 0:128]
    idx_s[WIN:168, :] = pack_tail(index_t[:, 128:144])

    def look_up(r, store):
        at = pl.multiple_of(r * 8, 8)
        entry = idx_s[pl.ds(at, 8), :]
        low = jnp.bitwise_and(entry, 127)
        high = jnp.right_shift(entry, 7)
        found = [jnp.zeros((8, 128), jnp.int32) for _ in range(6)]
        for k in range(26):
            here = high == k
            for h in range(6):
                line = jnp.broadcast_to(words_s[h:h + 1, 128 * k:128 * k + 128], (8, 128))
                got = jnp.take_along_axis(line, low, axis=1, mode="promise_in_bounds")
                found[h] = jnp.where(here, got, found[h])
        for h in range(6):
            store(h, at, jnp.right_shift(found[h], 16).astype(F32) * (1 / GRAIN))
            half = jnp.right_shift(jnp.left_shift(found[h], 16), 16)
            store(h + 6, at, half.astype(F32) * (1 / GRAIN))

    def main_rows(r, carry):
        def store(h, at, value):
            bias_s[h, pl.ds(at, 8), 0:128] = value
        look_up(r, store)
        return carry

    def tail_rows(r, carry):
        def store(h, at, value):
            tail_s[h, pl.ds(pl.multiple_of(at - WIN, 8), 8), :] = value
        look_up(r, store)
        return carry

    lax.fori_loop(0, 18, main_rows, 0)
    lax.fori_loop(18, 21, tail_rows, 0)

    def spread(h, carry):
        for at in range(0, WIN, 8):
            q, b = at // 64, at % 64 // 8
            bias_s[h, at:at + 8, 128:144] = tail_s[h, 8 * q:8 * q + 8, 16 * b:16 * b + 16]
        return carry

    lax.fori_loop(0, HEADS, spread, 0)
    gs_s[...] = jnp.zeros_like(gs_s)

    loads["reg"].wait()
    region = reg_ref[...].astype(F32).astype(BF16)
    col_of = lax.broadcasted_iota(jnp.int32, (24, WIN), 0)
    place = lax.broadcasted_iota(jnp.int32, (24, WIN), 1)
    row_of = lax.broadcasted_iota(jnp.int32, (6, WIN), 0)
    row_at = lax.rem(lax.broadcasted_iota(jnp.int32, (6, WIN), 1), 72) // 12
    allowed = []
    for w in range(2):
        choose = jnp.where(col_of == lax.rem(place, 12) + 12 * w, 1.0, 0.0).astype(BF16)
        line = jnp.sum(jnp.where(row_of == row_at, dot(region, choose), 0.0), axis=0, keepdims=True)
        down = jnp.broadcast_to(line, (128, WIN)).T
        allowed.append(down[:, 0:1] == line)

    loads["own"].wait()
    loads["put"].wait()
    mine = [dot(own_ref[...], ref[...]) for ref in (x_ref, c_ref)]

    def assemble(f, ref):
        for copy in arrive[3 * f:3 * f + 3]:
            copy.wait()
        ref[...] = (mine[f] + dot(put_ref[...], recv_in[f])).astype(BF16)

    assemble(0, xw_s)

    loads["wq"].wait()
    loads["wp"].wait()
    flat = xw_s[...].astype(F32)
    center = flat - jnp.mean(flat, axis=-1, keepdims=True)
    inverse = lax.rsqrt(jnp.mean(center * center, axis=-1, keepdims=True) + 1e-05)
    unit = center * inverse
    unit_s[...] = unit
    inv_s[...] = jnp.broadcast_to(inverse, inv_s.shape)
    normed = unit.astype(BF16)
    packed = dot(normed, wq_ref[...]).astype(BF16)
    for w in range(2):
        at = slice(WIN * w, WIN * w + WIN)
        qkv_s[w] = packed[at]
        qkvt_s[w] = packed[at].T
        normt_s[w] = normed[at].T
    assemble(1, cw_s)
    cot = cw_s[...]
    gm_s[...] = dot_nt(cot, wp_ref[...]).astype(BF16)
    for w in range(2):
        at = slice(WIN * w, WIN * w + WIN)
        gmt_s[w] = dot_nt(wp_ref[...], cot[at]).astype(BF16)

    lane = lax.broadcasted_iota(jnp.int32, (WIN, 128), 1)
    line_of = lax.broadcasted_iota(jnp.int32, (128, WIN), 0)

    for g in range(3):
        off = 128 * g
        grad_key = [None, None]
        grad_value = [None, None]
        for a in range(4):
            h = g * 4 + a
            own_line = (line_of >= 32 * a) & (line_of < 32 * a + 32)
            own_lane = (lane >= 32 * a) & (lane < 32 * a + 32)
            total = None
            bias = bias_s[h]
            for w in range(2):
                q = qkv_s[w, :, pl.ds(off, 128)]
                k = qkv_s[w, :, pl.ds(off + 384, 128)]
                v = qkv_s[w, :, pl.ds(off + 768, 128)]
                qt = qkvt_s[w, pl.ds(off, 128), :]
                gmt = gmt_s[w, pl.ds(off, 128), :]
                here = off + 32 * a
                kt = qkvt_s[w, pl.ds(384 + here, 32), :]
                vt = qkvt_s[w, pl.ds(768 + here, 32), :]
                gm = gm_s[pl.ds(WIN * w, WIN), pl.ds(off, 128)]
                zero = jnp.zeros((), BF16)
                s = dot(k, jnp.where(own_line, qt, zero)) * FACTOR + bias
                s = jnp.where(allowed[w], s, -1e30)
                e = jnp.exp(s - jnp.max(s, axis=0, keepdims=True))
                p = e * (1.0 / jnp.sum(e, axis=0, keepdims=True))
                pb = p.astype(BF16)
                mixt_s[w, pl.ds(here, 32), :] = dot(vt, pb).astype(BF16)
                gpr = dot(v, jnp.where(own_line, gmt, zero))
                gv = dot(pb, gm)
                gs = p * (gpr - jnp.sum(p * gpr, axis=0, keepdims=True))
                sc = (gs * FACTOR).astype(BF16)
                gqt_s[w, pl.ds(here, 32), :] = dot(kt, sc).astype(BF16)
                gk = dot(sc, q)
                grad_key[w] = gk if a == 0 else jnp.where(own_lane, gk, grad_key[w])
                grad_value[w] = gv if a == 0 else jnp.where(own_lane, gv, grad_value[w])
                total = gs if w == 0 else total + gs
            at = slice(h % 6, h % 6 + 1)
            gs_s[h // 6, 0:WIN, at, :] = total[:, 0:128].reshape(WIN, 1, 128)
            gs_s[h // 6, WIN:168, at, :] = pack_tail(total[:, 128:144]).reshape(24, 1, 128)
        for w in range(2):
            rows = slice(WIN * w, WIN * w + WIN)
            gp_s[rows, pl.ds(off + 384, 128)] = grad_key[w].astype(BF16)
            gp_s[rows, pl.ds(off + 768, 128)] = grad_value[w].astype(BF16)

    gs_send[...] = gs_s[1 - lev].reshape(1344, 128).astype(BF16)
    swap = push(gs_send, gs_recv, gs_ss.at[0], gs_rs.at[0], core_peer)

    for w in range(2):
        gp_s[WIN * w:WIN * w + WIN, 0:384] = gqt_s[w].T
    for half in range(2):
        part = [dot(normt_s[w], gp_s[WIN * w:WIN * w + WIN, 576 * half:576 * half + 576]) for w in range(2)]
        g_s[half, :, 0:576] = part[0] + part[1]
        part = [dot(mixt_s[w], cw_s[WIN * w:WIN * w + WIN, 192 * half:192 * half + 192]) for w in range(2)]
        g_s[half, :, 576:768] = part[0] + part[1]
    gsend[...] = g_s[1 - lev].astype(BF16)
    lat_rows = [pl.ds(pl.multiple_of(48 * step(lat, d, nlat), 48), 48) for d in range(1, nlat + 1)]
    core = [push(gsend.at[rows], gcore.at[rows], core_ss.at[n], core_rs.at[n], core_peer)
            for n, rows in enumerate(lat_rows)]

    loads["put_t"].wait()
    halo = []

    def halo_out(f, ref):
        send[f] = dot(put_t_ref[...], ref[...]).astype(BF16)
        for n, (at, size) in enumerate(PIECES):
            halo.append(push(send.at[f, pl.ds(at, size)], recv.at[f, pl.ds(at, size)],
                             halo_ss.at[3 * f + n], halo_rs.at[3 * f + n], after[n]))

    for w in range(2):
        branch_s[WIN * w:WIN * w + WIN, :] = dot(mixt_s[w].T, wp_ref[...]).astype(BF16)

    over_lat = []
    for n in range(nlat - 1):
        core[n].wait()
        lat_send[n] = (g_s[lev, lat_rows[n], :] + gcore[lat_rows[n], :].astype(F32)).astype(BF16)
        over_lat.append(push(lat_send.at[n], lat_recv.at[n], lat_ss.at[n], lat_rs.at[n], lat_peers[n]))
    core[nlat - 1].wait()
    halo_out(0, branch_s)

    gn = dot_nt(gp_s[...], wq_ref[...])
    unit = unit_s[...]
    rows_s[...] = (inv_s[:, 0:1] * (
        gn - jnp.mean(gn, axis=-1, keepdims=True)
        - unit * jnp.mean(gn * unit, axis=-1, keepdims=True))).astype(BF16)
    halo_out(1, rows_s)

    acc_s[...] = jnp.zeros_like(acc_s)
    low_of = lax.broadcasted_iota(jnp.int32, (256, 128), 0)

    def pairs(r, carry):
        entry = idx_s[pl.ds(pl.multiple_of(r * 8, 8), 8), :]
        low = jnp.bitwise_and(entry, 255)
        high = jnp.right_shift(entry, 8)
        other = gs_recv[pl.ds(pl.multiple_of(r * 64, 64), 64), :].astype(F32)
        both = gs_s[lev, pl.ds(r * 8, 8)] + other.reshape(8, 8, 128)
        lefts = []
        rights = []
        for s in range(8):
            value = both[s]
            lefts.append(jnp.concatenate(
                [jnp.where(high[s:s + 1, :] == k, value, 0.0) for k in range(13)], 0).astype(BF16))
            rights.append(jnp.where(low[s:s + 1, :] == low_of, 1.0, 0.0).astype(BF16))
        acc_s[...] += dot_nt(jnp.concatenate(lefts, 1), jnp.concatenate(rights, 1))
        return carry

    swap.wait()
    lax.fori_loop(0, 21, pairs, 0, unroll=3)
    tpart[...] = jnp.zeros_like(tpart)
    for k in range(13):
        tpart[16 * k:16 * k + 8, :] = acc_s[8 * k:8 * k + 8, 0:128]
        tpart[16 * k + 8:16 * k + 16, :] = acc_s[8 * k:8 * k + 8, 128:256]
    tsend[...] = tpart[...].astype(BF16)
    table = [push(tsend.at[pl.ds(pl.multiple_of(32 * step(y, d, 8), 32), 32)],
                  trecv.at[d - 1], t_ss.at[d - 1], t_rs.at[d - 1], y_peers[d - 1])
             for d in range(1, 8)]

    part = tpart[pl.ds(pl.multiple_of(32 * y, 32), 32), :]
    for n in range(7):
        table[n].wait()
        part = part + trecv[n].astype(F32)
    tz[z] = part
    over_z = [push(tz.at[z], tz.at[z], tz_ss.at[n], tz_rs.at[n], z_peers[n]) for n in range(nz - 1)]

    total = g_s[lev, lat_rows[-1], :] + gcore[lat_rows[-1], :].astype(F32)
    for n in range(nlat - 1):
        over_lat[n].wait()
        total = total + lat_recv[n].astype(F32)
    turn[...] = jnp.zeros_like(turn)
    turn[0:48, :] = total
    turn[64:112, :] = total
    turned[...] = turn[...].T
    first = lax.broadcasted_iota(jnp.int32, (24, 128), 1) < 64
    for to in range(8):
        for p in range(nz // 2):
            a, b = 16 * p + to, 16 * p + 8 + to
            ypart[to, 24 * p:24 * p + 18, :] = jnp.where(
                first[0:18], turned[18 * a:18 * a + 18, :], turned[18 * b:18 * b + 18, :])
            ypart[to, 24 * p + 18:24 * p + 24, :] = jnp.where(
                first[0:6], turned[576 + 6 * a:576 + 6 * a + 6, :], turned[576 + 6 * b:576 + 6 * b + 6, :])
    ysend[...] = ypart[...].astype(BF16)
    over_y = [push(ysend.at[step(y, d, 8)], yrecv.at[d - 1], y_ss.at[d - 1], y_rs.at[d - 1], y_peers[d - 1])
              for d in range(1, 8)]

    for copy in over_z:
        copy.wait()
    part = tz[0]
    for n in range(1, nz):
        part = part + tz[n]
    own_block = pl.ds(pl.multiple_of(32 * owner, 32), 32)
    tfull[own_block, :] = part.astype(BF16)
    gathered = [push(tfull.at[own_block], tfull.at[own_block], tg_ss.at[n], tg_rs.at[n], owners[n])
                for n in range(15)]

    total = ypart[y]
    for n in range(7):
        over_y[n].wait()
        total = total + yrecv[n].astype(F32)
    zpart[...] = total
    last = [push(zpart.at[pl.ds(pl.multiple_of(24 * (step(z, d, nz) // 2), 24), 24)],
                 zrecv.at[d - 1], z_ss.at[d - 1], z_rs.at[d - 1], z_peers[d - 1])
            for d in range(1, nz)]

    loads["own_t"].wait()
    loads["take_t"].wait()
    for f, (base, ref, out) in enumerate(((x_ref, branch_s, xo_ref), (c_ref, rows_s, co_ref))):
        for copy in halo[3 * f:3 * f + 3]:
            copy.wait()
        rolled = dot(own_t_ref[...], ref[...]) + dot(take_t_ref[...], recv[f])
        out[...] = (base[...].astype(F32) + rolled).astype(BF16)

    total = zpart[pl.ds(pl.multiple_of(24 * (z // 2), 24), 24), :]
    for n in range(nz - 1):
        last[n].wait()
        total = total + zrecv[n]
    total = jnp.where(lax.rem(z, 2) == 0, total[:, 0:48], total[:, 64:112]) * norm
    gq_ref[...] = total[0:18]
    gp_ref[...] = total[18:24]

    for n in range(15):
        gathered[n].wait()
    full = tfull[...].astype(F32)
    for k in range(26):
        width = min(128, POS - 128 * k)
        for h in range(HEADS):
            at = 256 * (h // 6) + 8 * k + h % 6
            to_ref[h, :, 128 * k:128 * k + width] = full[at:at + 1, 0:width]


def block(nlat, nlon, norm, *operands):
    nz = nlon // 8
    sem = pltpu.SemaphoreType.DMA
    vmem = pltpu.VMEM
    loaded = [operands[n] for n in range(13)]
    return pl.pallas_call(
        functools.partial(block_kernel, nlat, nlon, norm),
        in_specs=[pl.BlockSpec(memory_space=pl.ANY)] * 13,
        out_shape=[
            jax.ShapeDtypeStruct((288, 384), BF16),
            jax.ShapeDtypeStruct((288, 384), BF16),
            jax.ShapeDtypeStruct((18, 48), F32),
            jax.ShapeDtypeStruct((6, 48), F32),
            jax.ShapeDtypeStruct((HEADS, 1, POS), F32),
        ],
        scratch_shapes=[vmem(a.shape, a.dtype) for a in loaded] + [
            vmem((288, 384), BF16),
            vmem((288, 384), BF16),
            vmem((8, 3328), jnp.int32),
            vmem((16, POS), F32),
            vmem((168, 128), jnp.int32),
            vmem((12, 24, 128), F32),
            vmem((12, 144, 144), F32),
            vmem((2, 144, 1152), BF16),
            vmem((2, 1152, 144), BF16),
            vmem((288, 384), BF16),
            vmem((2, 384, 144), BF16),
            vmem((2, 384, 144), BF16),
            vmem((2, 384, 144), BF16),
            vmem((288, 1152), BF16),
            vmem((288, 384), F32),
            vmem((288, 128), F32),
            vmem((2, 384, 144), BF16),
            vmem((2, 168, 8, 128), F32),
            vmem((104, 256), F32),
            vmem((288, 384), BF16),
            vmem((288, 384), BF16),
            vmem((2, 384, 768), F32),
            vmem((256, 128), F32),
            vmem((2, 208, 384), BF16),
            vmem((2, 208, 384), BF16),
            vmem((2, 208, 384), BF16),
            vmem((2, 208, 384), BF16),
            vmem((384, 768), BF16),
            vmem((384, 768), BF16),
            vmem((nlat - 1, 48, 768), BF16),
            vmem((nlat - 1, 48, 768), BF16),
            vmem((128, 768), F32),
            vmem((768, 128), F32),
            vmem((8, 48, 128), F32),
            vmem((8, 48, 128), BF16),
            vmem((7, 48, 128), BF16),
            vmem((48, 128), F32),
            vmem((nz - 1, 24, 128), F32),
            vmem((1344, 128), BF16),
            vmem((1344, 128), BF16),
            vmem((256, 128), BF16),
            vmem((7, 32, 128), BF16),
            vmem((nz, 32, 128), F32),
            vmem((512, 128), BF16),
            sem((13,)), sem((6,)), sem((6,)), sem((6,)), sem((6,)), sem((nlat,)), sem((nlat,)),
            sem((nlat - 1,)), sem((nlat - 1,)),
            sem((7,)), sem((7,)), sem((nz - 1,)), sem((nz - 1,)),
            sem((7,)), sem((7,)), sem((nz - 1,)), sem((nz - 1,)), sem((15,)), sem((15,)), sem((1,)), sem((1,)),
        ],
        compiler_params=pltpu.CompilerParams(
            collective_id=0, has_side_effects=True, vmem_limit_bytes=56 * 1024 * 1024),
        name="block",
    )(*operands)


def publish_kernel(*refs):
    results, outs, held = refs[0:5], refs[5:10], refs[10:15]
    in_sem, out_sem = refs[15:]
    loads = [pltpu.make_async_copy(results[n], held[n], in_sem.at[n]) for n in range(5)]
    stores = [pltpu.make_async_copy(held[n], outs[n], out_sem.at[n]) for n in range(5)]
    for copy in loads:
        copy.start()
    for n in range(5):
        loads[n].wait()
        stores[n].start()
    for copy in stores:
        copy.wait()


def publish(*results):
    sem = pltpu.SemaphoreType.DMA
    return pl.pallas_call(
        publish_kernel,
        in_specs=[pl.BlockSpec(memory_space=pl.ANY)] * 5,
        out_specs=[pl.BlockSpec(memory_space=pl.ANY)] * 5,
        out_shape=[jax.ShapeDtypeStruct(r.shape, r.dtype) for r in results],
        scratch_shapes=[pltpu.VMEM(r.shape, r.dtype) for r in results] + [sem((5,)), sem((5,))],
        compiler_params=pltpu.CompilerParams(vmem_limit_bytes=56 * 1024 * 1024),
        name="publish",
    )(*results)


def body(tokens, cotangent, w_qkv, w_proj, bias_table, bias_index, region_ids):
    levels, rows, columns, width = tokens.shape
    nlev, nlat, nlon = lax.axis_size("lev"), lax.axis_size("lat"), lax.axis_size("lon")
    norm = 1.0 / math.sqrt(levels * nlev * rows * nlat * columns * nlon)
    send, own, recv = permutations()
    send, own, recv, send_t, own_t, recv_t = [
        jnp.asarray(m, BF16) for m in (send, own, recv, send.T, own.T, recv.T)]
    results = block(
        nlat, nlon, norm, tokens.reshape(288, width), cotangent.reshape(288, width), w_qkv, w_proj,
        bias_table.transpose(1, 0, 2), bias_index[0], region_ids, send, own, recv, send_t, own_t, recv_t)
    block_out, grad_tokens, gq, gp, table = publish(*results)
    return (block_out.reshape(tokens.shape), grad_tokens.reshape(tokens.shape), gq.T, gp.T,
            table.transpose(1, 0, 2))


def solution(mesh):
    return jax.shard_map(
        body,
        mesh=mesh,
        in_specs=(
            jax.P("lev", "lat", "lon", None),
            jax.P("lev", "lat", "lon", None),
            jax.P(),
            jax.P(),
            jax.P("lat", None, None),
            jax.P("lat", None, None),
            jax.P("lat", "lon"),
        ),
        out_specs=(
            jax.P("lev", "lat", "lon", None),
            jax.P("lev", "lat", "lon", None),
            jax.P("lat", ("lev", "lon")),
            jax.P("lat", ("lev", "lon")),
            jax.P("lat", None, None),
        ),
        check_vma=False,
    )
```

```python
import functools
import math

import jax
import jax.numpy as jnp
import numpy as np
from jax import lax
from jax.experimental import pallas as pl
from jax.experimental.pallas import tpu as pltpu

F32 = jnp.float32
BF16 = jnp.bfloat16
HEADS = 12
WIN = 144
WIDTH = 384
POS = 3312
GRAIN = 32767 / 5
FACTOR = 32 ** (-0.5)


def dot(a, b):
    return lax.dot_general(a, b, (((1,), (0,)), ((), ())), preferred_element_type=F32)


def dot_nt(a, b):
    return lax.dot_general(a, b, (((1,), (1,)), ((), ())), preferred_element_type=F32)


def pack_tail(block):
    rows = []
    for q in range(3):
        parts = []
        for b in range(8):
            at = 64 * q + 8 * b
            if at < WIN:
                parts.append(block[at:at + 8, :])
            else:
                parts.append(jnp.full((8, 16), -1, block.dtype))
        rows.append(jnp.concatenate(parts, 1))
    return jnp.concatenate(rows, 0)


PIECES = ((0, 112), (112, 48), (160, 48))
MESH = pl.DeviceIdType.MESH


@functools.lru_cache(None)
def permutations():
    place = {}
    for l in range(2):
        for r in range(3):
            for c in range(6, 24):
                place[l, r, c] = l * 54 + r * 18 + c - 6
        for r in range(3, 6):
            for c in range(6):
                place[l, r, c] = 112 + l * 18 + (r - 3) * 6 + c
        for r in range(3):
            for c in range(6):
                place[l, r, c] = 160 + l * 18 + r * 6 + c
    send = np.zeros((208, 288), np.float32)
    for (l, r, c), at in place.items():
        send[at, l * 144 + r * 24 + c] = 1
    own = np.zeros((288, 288), np.float32)
    recv = np.zeros((288, 208), np.float32)
    for w in range(2):
        for l in range(2):
            for r in range(6):
                for c in range(12):
                    row = w * 144 + l * 72 + r * 12 + c
                    at, col = r + 3, 12 * w + c + 6
                    if at < 6 and col < 24:
                        own[row, l * 144 + at * 24 + col] = 1
                    else:
                        recv[row, place[l, at % 6, col % 24]] = 1
    return send, own, recv


def step(index, by, count):
    return lax.rem(index + (by + count), count)


def block_kernel(nlat, nlon, norm, x_hbm, c_hbm, wq_hbm, wp_hbm, tab_hbm, idx_hbm, reg_hbm,
                 take_hbm, own_hbm, put_hbm, take_t_hbm, own_t_hbm, put_t_hbm,
                 xo_ref, co_ref, gq_ref, gp_ref, to_ref,
                 x_ref, c_ref, wq_ref, wp_ref, tab_ref, idx_ref, reg_ref,
                 take_ref, own_ref, put_ref, take_t_ref, own_t_ref, put_t_ref,
                 xw_s, cw_s, words_s, rows_of_table, idx_s, tail_s, bias_s, qkv_s, qkvt_s, gm_s, gmt_s, mixt_s, gqt_s, gp_s,
                 unit_s, inv_s, normt_s, gs_s, acc_s, branch_s, rows_s, g_s, tpart,
                 send_in, recv_in, send, recv, gsend, gcore, lat_send, lat_recv, turn, turned, ypart, ysend, yrecv,
                 zpart, zrecv, gs_send, gs_recv, tsend, trecv, tz, tfull,
                 load_sem, in_ss, in_rs, halo_ss, halo_rs, core_ss, core_rs, lat_ss, lat_rs,
                 y_ss, y_rs, z_ss, z_rs, t_ss, t_rs, tz_ss, tz_rs, tg_ss, tg_rs, gs_ss, gs_rs):
    nz = nlon // 8
    lev, lat, lon = lax.axis_index("lev"), lax.axis_index("lat"), lax.axis_index("lon")
    z, y = lon // 8, lax.rem(lon, 8)
    owner = lev * 8 + y

    def at_owner(o):
        return {"lev": o // 8, "lat": lat, "lon": z * 8 + lax.rem(o, 8)}

    core_peer = {"lev": 1 - lev, "lat": lat, "lon": lon}
    lat_peers = [{"lev": lev, "lat": step(lat, d, nlat), "lon": lon} for d in range(1, nlat)]
    y_peers = [{"lev": lev, "lat": lat, "lon": z * 8 + step(y, d, 8)} for d in range(1, 8)]
    z_peers = [{"lev": lev, "lat": lat, "lon": step(z, d, nz) * 8 + y} for d in range(1, nz)]
    owners = [at_owner(step(owner, d, 16)) for d in range(1, 16)]
    after, before = [
        [{"lev": lev, "lat": step(lat, by, nlat), "lon": lon},
         {"lev": lev, "lat": lat, "lon": step(lon, by, nlon)},
         {"lev": lev, "lat": step(lat, by, nlat), "lon": step(lon, by, nlon)}] for by in (1, -1)]
    barrier = pltpu.get_barrier_semaphore()
    greet = after[1:] + before[1:] + lat_peers + owners + z_peers
    for device in greet:
        pl.semaphore_signal(barrier, inc=1, device_id=device, device_id_type=MESH)

    names = ("x", "c", "take", "own", "put", "tab", "idx", "reg", "wq", "wp", "own_t", "take_t", "put_t")
    from_to = ((x_hbm, x_ref), (c_hbm, c_ref), (take_hbm, take_ref), (own_hbm, own_ref), (put_hbm, put_ref),
                (tab_hbm, tab_ref), (idx_hbm, idx_ref), (reg_hbm, reg_ref), (wq_hbm, wq_ref), (wp_hbm, wp_ref),
                (own_t_hbm, own_t_ref), (take_t_hbm, take_t_ref), (put_t_hbm, put_t_ref))
    loads = {}
    for n, (name, (src, dst)) in enumerate(zip(names, from_to)):
        loads[name] = pltpu.make_async_copy(src, dst, load_sem.at[n])
        loads[name].start()

    def push(src, dst, ss, rs, device):
        copy = pltpu.make_async_remote_copy(
            src_ref=src, dst_ref=dst, send_sem=ss, recv_sem=rs, device_id=device, device_id_type=MESH)
        copy.start()
        return copy

    for name in ("x", "c", "take"):
        loads[name].wait()
    for f, ref in enumerate((x_ref, c_ref)):
        send_in[f] = dot(take_ref[...], ref[...]).astype(BF16)
    pl.semaphore_wait(barrier, len(greet))
    arrive = [push(send_in.at[f, pl.ds(at, size)], recv_in.at[f, pl.ds(at, size)],
                   in_ss.at[3 * f + n], in_rs.at[3 * f + n], before[n])
              for f in range(2) for n, (at, size) in enumerate(PIECES)]

    for name in ("tab", "idx"):
        loads[name].wait()
    words_s[...] = jnp.zeros_like(words_s)
    for h in range(HEADS):
        rows_of_table[h:h + 1, :] = tab_ref[h]
    upper = jnp.floor(rows_of_table[0:6, :] * GRAIN + 0.5).astype(jnp.int32)
    lower = jnp.floor(rows_of_table[6:12, :] * GRAIN + 0.5).astype(jnp.int32)
    words_s[0:6, 0:POS] = jnp.left_shift(upper, 16) + jnp.bitwise_and(lower, 65535)
    index_t = idx_ref[...].T
    idx_s[0:WIN, :] = index_t[:, 0:128]
    idx_s[WIN:168, :] = pack_tail(index_t[:, 128:144])

    def look_up(r, store):
        at = pl.multiple_of(r * 8, 8)
        entry = idx_s[pl.ds(at, 8), :]
        low = jnp.bitwise_and(entry, 127)
        high = jnp.right_shift(entry, 7)
        found = [jnp.zeros((8, 128), jnp.int32) for _ in range(6)]
        for k in range(26):
            here = high == k
            for h in range(6):
                line = jnp.broadcast_to(words_s[h:h + 1, 128 * k:128 * k + 128], (8, 128))
                got = jnp.take_along_axis(line, low, axis=1, mode="promise_in_bounds")
                found[h] = jnp.where(here, got, found[h])
        for h in range(6):
            store(h, at, jnp.right_shift(found[h], 16).astype(F32) * (1 / GRAIN))
            half = jnp.right_shift(jnp.left_shift(found[h], 16), 16)
            store(h + 6, at, half.astype(F32) * (1 / GRAIN))

    def main_rows(r, carry):
        def store(h, at, value):
            bias_s[h, pl.ds(at, 8), 0:128] = value
        look_up(r, store)
        return carry

    def tail_rows(r, carry):
        def store(h, at, value):
            tail_s[h, pl.ds(pl.multiple_of(at - WIN, 8), 8), :] = value
        look_up(r, store)
        return carry

    lax.fori_loop(0, 18, main_rows, 0)
    lax.fori_loop(18, 21, tail_rows, 0)

    def spread(h, carry):
        for at in range(0, WIN, 8):
            q, b = at // 64, at % 64 // 8
            bias_s[h, at:at + 8, 128:144] = tail_s[h, 8 * q:8 * q + 8, 16 * b:16 * b + 16]
        return carry

    lax.fori_loop(0, HEADS, spread, 0)
    gs_s[...] = jnp.zeros_like(gs_s)

    loads["reg"].wait()
    region = reg_ref[...].astype(F32).astype(BF16)
    col_of = lax.broadcasted_iota(jnp.int32, (24, WIN), 0)
    place = lax.broadcasted_iota(jnp.int32, (24, WIN), 1)
    row_of = lax.broadcasted_iota(jnp.int32, (6, WIN), 0)
    row_at = lax.rem(lax.broadcasted_iota(jnp.int32, (6, WIN), 1), 72) // 12
    allowed = []
    for w in range(2):
        choose = jnp.where(col_of == lax.rem(place, 12) + 12 * w, 1.0, 0.0).astype(BF16)
        line = jnp.sum(jnp.where(row_of == row_at, dot(region, choose), 0.0), axis=0, keepdims=True)
        down = jnp.broadcast_to(line, (128, WIN)).T
        allowed.append(down[:, 0:1] == line)

    loads["own"].wait()
    loads["put"].wait()
    mine = [dot(own_ref[...], ref[...]) for ref in (x_ref, c_ref)]

    def assemble(f, ref):
        for copy in arrive[3 * f:3 * f + 3]:
            copy.wait()
        ref[...] = (mine[f] + dot(put_ref[...], recv_in[f])).astype(BF16)

    assemble(0, xw_s)

    loads["wq"].wait()
    loads["wp"].wait()
    flat = xw_s[...].astype(F32)
    center = flat - jnp.mean(flat, axis=-1, keepdims=True)
    inverse = lax.rsqrt(jnp.mean(center * center, axis=-1, keepdims=True) + 1e-05)
    unit = center * inverse
    unit_s[...] = unit
    inv_s[...] = jnp.broadcast_to(inverse, inv_s.shape)
    normed = unit.astype(BF16)
    packed = dot(normed, wq_ref[...]).astype(BF16)
    for w in range(2):
        at = slice(WIN * w, WIN * w + WIN)
        qkv_s[w] = packed[at]
        qkvt_s[w] = packed[at].T
        normt_s[w] = normed[at].T
    assemble(1, cw_s)
    cot = cw_s[...]
    gm_s[...] = dot_nt(cot, wp_ref[...]).astype(BF16)
    for w in range(2):
        at = slice(WIN * w, WIN * w + WIN)
        gmt_s[w] = dot_nt(wp_ref[...], cot[at]).astype(BF16)

    lane = lax.broadcasted_iota(jnp.int32, (WIN, 128), 1)
    line_of = lax.broadcasted_iota(jnp.int32, (128, WIN), 0)

    for g in range(3):
        off = 128 * g
        grad_key = [None, None]
        grad_value = [None, None]
        for a in range(4):
            h = g * 4 + a
            own_line = (line_of >= 32 * a) & (line_of < 32 * a + 32)
            own_lane = (lane >= 32 * a) & (lane < 32 * a + 32)
            total = None
            bias = bias_s[h]
            for w in range(2):
                q = qkv_s[w, :, pl.ds(off, 128)]
                k = qkv_s[w, :, pl.ds(off + 384, 128)]
                v = qkv_s[w, :, pl.ds(off + 768, 128)]
                qt = qkvt_s[w, pl.ds(off, 128), :]
                gmt = gmt_s[w, pl.ds(off, 128), :]
                here = off + 32 * a
                kt = qkvt_s[w, pl.ds(384 + here, 32), :]
                vt = qkvt_s[w, pl.ds(768 + here, 32), :]
                gm = gm_s[pl.ds(WIN * w, WIN), pl.ds(off, 128)]
                zero = jnp.zeros((), BF16)
                s = dot(k, jnp.where(own_line, qt, zero)) * FACTOR + bias
                s = jnp.where(allowed[w], s, -1e30)
                e = jnp.exp(s - jnp.max(s, axis=0, keepdims=True))
                p = e * (1.0 / jnp.sum(e, axis=0, keepdims=True))
                pb = p.astype(BF16)
                mixt_s[w, pl.ds(here, 32), :] = dot(vt, pb).astype(BF16)
                gpr = dot(v, jnp.where(own_line, gmt, zero))
                gv = dot(pb, gm)
                gs = p * (gpr - jnp.sum(p * gpr, axis=0, keepdims=True))
                sc = (gs * FACTOR).astype(BF16)
                gqt_s[w, pl.ds(here, 32), :] = dot(kt, sc).astype(BF16)
                gk = dot(sc, q)
                grad_key[w] = gk if a == 0 else jnp.where(own_lane, gk, grad_key[w])
                grad_value[w] = gv if a == 0 else jnp.where(own_lane, gv, grad_value[w])
                total = gs if w == 0 else total + gs
            at = slice(h % 6, h % 6 + 1)
            gs_s[h // 6, 0:WIN, at, :] = total[:, 0:128].reshape(WIN, 1, 128)
            gs_s[h // 6, WIN:168, at, :] = pack_tail(total[:, 128:144]).reshape(24, 1, 128)
        for w in range(2):
            rows = slice(WIN * w, WIN * w + WIN)
            gp_s[rows, pl.ds(off + 384, 128)] = grad_key[w].astype(BF16)
            gp_s[rows, pl.ds(off + 768, 128)] = grad_value[w].astype(BF16)

    gs_send[...] = gs_s[1 - lev].reshape(1344, 128).astype(BF16)
    swap = push(gs_send, gs_recv, gs_ss.at[0], gs_rs.at[0], core_peer)

    for w in range(2):
        gp_s[WIN * w:WIN * w + WIN, 0:384] = gqt_s[w].T
    for half in range(2):
        part = [dot(normt_s[w], gp_s[WIN * w:WIN * w + WIN, 576 * half:576 * half + 576]) for w in range(2)]
        g_s[half, :, 0:576] = part[0] + part[1]
        part = [dot(mixt_s[w], cw_s[WIN * w:WIN * w + WIN, 192 * half:192 * half + 192]) for w in range(2)]
        g_s[half, :, 576:768] = part[0] + part[1]
    gsend[...] = g_s[1 - lev].astype(BF16)
    lat_rows = [pl.ds(pl.multiple_of(48 * step(lat, d, nlat), 48), 48) for d in range(1, nlat + 1)]
    core = [push(gsend.at[rows], gcore.at[rows], core_ss.at[n], core_rs.at[n], core_peer)
            for n, rows in enumerate(lat_rows)]

    loads["put_t"].wait()
    for w in range(2):
        branch_s[WIN * w:WIN * w + WIN, :] = dot(mixt_s[w].T, wp_ref[...]).astype(BF16)
    send[0] = dot(put_t_ref[...], branch_s[...]).astype(BF16)

    over_lat = []
    for n in range(nlat - 1):
        core[n].wait()
        lat_send[n] = (g_s[lev, lat_rows[n], :] + gcore[lat_rows[n], :].astype(F32)).astype(BF16)
        over_lat.append(push(lat_send.at[n], lat_recv.at[n], lat_ss.at[n], lat_rs.at[n], lat_peers[n]))
    core[nlat - 1].wait()

    acc_s[...] = jnp.zeros_like(acc_s)
    low_of = lax.broadcasted_iota(jnp.int32, (256, 128), 0)

    def pairs(r, carry):
        entry = idx_s[pl.ds(pl.multiple_of(r * 8, 8), 8), :]
        low = jnp.bitwise_and(entry, 255)
        high = jnp.right_shift(entry, 8)
        other = gs_recv[pl.ds(pl.multiple_of(r * 64, 64), 64), :].astype(F32)
        both = gs_s[lev, pl.ds(r * 8, 8)] + other.reshape(8, 8, 128)
        lefts = []
        rights = []
        for s in range(8):
            value = both[s]
            lefts.append(jnp.concatenate(
                [jnp.where(high[s:s + 1, :] == k, value, 0.0) for k in range(13)], 0).astype(BF16))
            rights.append(jnp.where(low[s:s + 1, :] == low_of, 1.0, 0.0).astype(BF16))
        acc_s[...] += dot_nt(jnp.concatenate(lefts, 1), jnp.concatenate(rights, 1))
        return carry

    swap.wait()
    lax.fori_loop(0, 21, pairs, 0, unroll=7)
    tpart[...] = jnp.zeros_like(tpart)
    for k in range(13):
        tpart[16 * k:16 * k + 8, :] = acc_s[8 * k:8 * k + 8, 0:128]
        tpart[16 * k + 8:16 * k + 16, :] = acc_s[8 * k:8 * k + 8, 128:256]
    tsend[...] = tpart[...].astype(BF16)
    table = [push(tsend.at[pl.ds(pl.multiple_of(32 * step(y, d, 8), 32), 32)],
                  trecv.at[d - 1], t_ss.at[d - 1], t_rs.at[d - 1], y_peers[d - 1])
             for d in range(1, 8)]

    def halo_out(f):
        return [push(send.at[f, pl.ds(at, size)], recv.at[f, pl.ds(at, size)],
                     halo_ss.at[3 * f + n], halo_rs.at[3 * f + n], after[n])
                for n, (at, size) in enumerate(PIECES)]

    halo = halo_out(0)
    gn = dot_nt(gp_s[...], wq_ref[...])
    unit = unit_s[...]
    rows_s[...] = (inv_s[:, 0:1] * (
        gn - jnp.mean(gn, axis=-1, keepdims=True)
        - unit * jnp.mean(gn * unit, axis=-1, keepdims=True))).astype(BF16)
    send[1] = dot(put_t_ref[...], rows_s[...]).astype(BF16)

    halo += halo_out(1)

    part = tpart[pl.ds(pl.multiple_of(32 * y, 32), 32), :]
    for n in range(7):
        table[n].wait()
        part = part + trecv[n].astype(F32)
    tz[z] = part
    over_z = [push(tz.at[z], tz.at[z], tz_ss.at[n], tz_rs.at[n], z_peers[n]) for n in range(nz - 1)]

    total = g_s[lev, lat_rows[-1], :] + gcore[lat_rows[-1], :].astype(F32)
    for n in range(nlat - 1):
        over_lat[n].wait()
        total = total + lat_recv[n].astype(F32)
    turn[...] = jnp.zeros_like(turn)
    turn[0:48, :] = total
    turn[64:112, :] = total
    turned[...] = turn[...].T
    first = lax.broadcasted_iota(jnp.int32, (24, 128), 1) < 64
    for to in range(8):
        for p in range(nz // 2):
            a, b = 16 * p + to, 16 * p + 8 + to
            ypart[to, 24 * p:24 * p + 18, :] = jnp.where(
                first[0:18], turned[18 * a:18 * a + 18, :], turned[18 * b:18 * b + 18, :])
            ypart[to, 24 * p + 18:24 * p + 24, :] = jnp.where(
                first[0:6], turned[576 + 6 * a:576 + 6 * a + 6, :], turned[576 + 6 * b:576 + 6 * b + 6, :])
    ysend[...] = ypart[...].astype(BF16)
    over_y = [push(ysend.at[step(y, d, 8)], yrecv.at[d - 1], y_ss.at[d - 1], y_rs.at[d - 1], y_peers[d - 1])
              for d in range(1, 8)]

    for copy in over_z:
        copy.wait()
    part = tz[0]
    for n in range(1, nz):
        part = part + tz[n]
    own_block = pl.ds(pl.multiple_of(32 * owner, 32), 32)
    tfull[own_block, :] = part.astype(BF16)
    gathered = [push(tfull.at[own_block], tfull.at[own_block], tg_ss.at[n], tg_rs.at[n], owners[n])
                for n in range(15)]

    total = ypart[y]
    for n in range(7):
        over_y[n].wait()
        total = total + yrecv[n].astype(F32)
    zpart[...] = total
    last = [push(zpart.at[pl.ds(pl.multiple_of(24 * (step(z, d, nz) // 2), 24), 24)],
                 zrecv.at[d - 1], z_ss.at[d - 1], z_rs.at[d - 1], z_peers[d - 1])
            for d in range(1, nz)]

    loads["own_t"].wait()
    loads["take_t"].wait()
    for f, (base, ref, out) in enumerate(((x_ref, branch_s, xo_ref), (c_ref, rows_s, co_ref))):
        for copy in halo[3 * f:3 * f + 3]:
            copy.wait()
        rolled = dot(own_t_ref[...], ref[...]) + dot(take_t_ref[...], recv[f])
        out[...] = (base[...].astype(F32) + rolled).astype(BF16)

    total = zpart[pl.ds(pl.multiple_of(24 * (z // 2), 24), 24), :]
    for n in range(nz - 1):
        last[n].wait()
        total = total + zrecv[n]
    total = jnp.where(lax.rem(z, 2) == 0, total[:, 0:48], total[:, 64:112]) * norm
    gq_ref[...] = total[0:18]
    gp_ref[...] = total[18:24]

    for n in range(15):
        gathered[n].wait()
    full = tfull[...].astype(F32)
    for k in range(26):
        width = min(128, POS - 128 * k)
        for h in range(HEADS):
            at = 256 * (h // 6) + 8 * k + h % 6
            to_ref[h, :, 128 * k:128 * k + width] = full[at:at + 1, 0:width]


def block(nlat, nlon, norm, *operands):
    nz = nlon // 8
    sem = pltpu.SemaphoreType.DMA
    vmem = pltpu.VMEM
    loaded = [operands[n] for n in range(13)]
    return pl.pallas_call(
        functools.partial(block_kernel, nlat, nlon, norm),
        in_specs=[pl.BlockSpec(memory_space=pl.ANY)] * 13,
        out_shape=[
            jax.ShapeDtypeStruct((288, 384), BF16),
            jax.ShapeDtypeStruct((288, 384), BF16),
            jax.ShapeDtypeStruct((18, 48), F32),
            jax.ShapeDtypeStruct((6, 48), F32),
            jax.ShapeDtypeStruct((HEADS, 1, POS), F32),
        ],
        scratch_shapes=[vmem(a.shape, a.dtype) for a in loaded] + [
            vmem((288, 384), BF16),
            vmem((288, 384), BF16),
            vmem((8, 3328), jnp.int32),
            vmem((16, POS), F32),
            vmem((168, 128), jnp.int32),
            vmem((12, 24, 128), F32),
            vmem((12, 144, 144), F32),
            vmem((2, 144, 1152), BF16),
            vmem((2, 1152, 144), BF16),
            vmem((288, 384), BF16),
            vmem((2, 384, 144), BF16),
            vmem((2, 384, 144), BF16),
            vmem((2, 384, 144), BF16),
            vmem((288, 1152), BF16),
            vmem((288, 384), F32),
            vmem((288, 128), F32),
            vmem((2, 384, 144), BF16),
            vmem((2, 168, 8, 128), F32),
            vmem((104, 256), F32),
            vmem((288, 384), BF16),
            vmem((288, 384), BF16),
            vmem((2, 384, 768), F32),
            vmem((256, 128), F32),
            vmem((2, 208, 384), BF16),
            vmem((2, 208, 384), BF16),
            vmem((2, 208, 384), BF16),
            vmem((2, 208, 384), BF16),
            vmem((384, 768), BF16),
            vmem((384, 768), BF16),
            vmem((nlat - 1, 48, 768), BF16),
            vmem((nlat - 1, 48, 768), BF16),
            vmem((128, 768), F32),
            vmem((768, 128), F32),
            vmem((8, 48, 128), F32),
            vmem((8, 48, 128), BF16),
            vmem((7, 48, 128), BF16),
            vmem((48, 128), F32),
            vmem((nz - 1, 24, 128), F32),
            vmem((1344, 128), BF16),
            vmem((1344, 128), BF16),
            vmem((256, 128), BF16),
            vmem((7, 32, 128), BF16),
            vmem((nz, 32, 128), F32),
            vmem((512, 128), BF16),
            sem((13,)), sem((6,)), sem((6,)), sem((6,)), sem((6,)), sem((nlat,)), sem((nlat,)),
            sem((nlat - 1,)), sem((nlat - 1,)),
            sem((7,)), sem((7,)), sem((nz - 1,)), sem((nz - 1,)),
            sem((7,)), sem((7,)), sem((nz - 1,)), sem((nz - 1,)), sem((15,)), sem((15,)), sem((1,)), sem((1,)),
        ],
        compiler_params=pltpu.CompilerParams(
            collective_id=0, has_side_effects=True, vmem_limit_bytes=56 * 1024 * 1024),
        name="block",
    )(*operands)


def publish_kernel(*refs):
    results, outs, held = refs[0:5], refs[5:10], refs[10:15]
    in_sem, out_sem = refs[15:]
    loads = [pltpu.make_async_copy(results[n], held[n], in_sem.at[n]) for n in range(5)]
    stores = [pltpu.make_async_copy(held[n], outs[n], out_sem.at[n]) for n in range(5)]
    for copy in loads:
        copy.start()
    for n in range(5):
        loads[n].wait()
        stores[n].start()
    for copy in stores:
        copy.wait()


def publish(*results):
    sem = pltpu.SemaphoreType.DMA
    return pl.pallas_call(
        publish_kernel,
        in_specs=[pl.BlockSpec(memory_space=pl.ANY)] * 5,
        out_specs=[pl.BlockSpec(memory_space=pl.ANY)] * 5,
        out_shape=[jax.ShapeDtypeStruct(r.shape, r.dtype) for r in results],
        scratch_shapes=[pltpu.VMEM(r.shape, r.dtype) for r in results] + [sem((5,)), sem((5,))],
        compiler_params=pltpu.CompilerParams(vmem_limit_bytes=56 * 1024 * 1024),
        name="publish",
    )(*results)


def body(tokens, cotangent, w_qkv, w_proj, bias_table, bias_index, region_ids):
    levels, rows, columns, width = tokens.shape
    nlev, nlat, nlon = lax.axis_size("lev"), lax.axis_size("lat"), lax.axis_size("lon")
    norm = 1.0 / math.sqrt(levels * nlev * rows * nlat * columns * nlon)
    send, own, recv = permutations()
    send, own, recv, send_t, own_t, recv_t = [
        jnp.asarray(m, BF16) for m in (send, own, recv, send.T, own.T, recv.T)]
    results = block(
        nlat, nlon, norm, tokens.reshape(288, width), cotangent.reshape(288, width), w_qkv, w_proj,
        bias_table.transpose(1, 0, 2), bias_index[0], region_ids, send, own, recv, send_t, own_t, recv_t)
    block_out, grad_tokens, gq, gp, table = publish(*results)
    return (block_out.reshape(tokens.shape), grad_tokens.reshape(tokens.shape), gq.T, gp.T,
            table.transpose(1, 0, 2))


def solution(mesh):
    return jax.shard_map(
        body,
        mesh=mesh,
        in_specs=(
            jax.P("lev", "lat", "lon", None),
            jax.P("lev", "lat", "lon", None),
            jax.P(),
            jax.P(),
            jax.P("lat", None, None),
            jax.P("lat", None, None),
            jax.P("lat", "lon"),
        ),
        out_specs=(
            jax.P("lev", "lat", "lon", None),
            jax.P("lev", "lat", "lon", None),
            jax.P("lat", ("lev", "lon")),
            jax.P("lat", ("lev", "lon")),
            jax.P("lat", None, None),
        ),
        check_vma=False,
    )
```

```python
import functools
import math

import jax
import jax.numpy as jnp
import numpy as np
from jax import lax
from jax.experimental import pallas as pl
from jax.experimental.pallas import tpu as pltpu

F32 = jnp.float32
BF16 = jnp.bfloat16
HEADS = 12
WIN = 144
WIDTH = 384
POS = 3312
GRAIN = 32767 / 5
FACTOR = 32 ** (-0.5)


def dot(a, b):
    return lax.dot_general(a, b, (((1,), (0,)), ((), ())), preferred_element_type=F32)


def dot_nt(a, b):
    return lax.dot_general(a, b, (((1,), (1,)), ((), ())), preferred_element_type=F32)


def pack_tail(block):
    rows = []
    for q in range(3):
        parts = []
        for b in range(8):
            at = 64 * q + 8 * b
            if at < WIN:
                parts.append(block[at:at + 8, :])
            else:
                parts.append(jnp.full((8, 16), -1, block.dtype))
        rows.append(jnp.concatenate(parts, 1))
    return jnp.concatenate(rows, 0)


PIECES = ((0, 112), (112, 48), (160, 48))
MESH = pl.DeviceIdType.MESH


@functools.lru_cache(None)
def permutations():
    place = {}
    for l in range(2):
        for r in range(3):
            for c in range(6, 24):
                place[l, r, c] = l * 54 + r * 18 + c - 6
        for r in range(3, 6):
            for c in range(6):
                place[l, r, c] = 112 + l * 18 + (r - 3) * 6 + c
        for r in range(3):
            for c in range(6):
                place[l, r, c] = 160 + l * 18 + r * 6 + c
    send = np.zeros((208, 288), np.float32)
    for (l, r, c), at in place.items():
        send[at, l * 144 + r * 24 + c] = 1
    own = np.zeros((288, 288), np.float32)
    recv = np.zeros((288, 208), np.float32)
    for w in range(2):
        for l in range(2):
            for r in range(6):
                for c in range(12):
                    row = w * 144 + l * 72 + r * 12 + c
                    at, col = r + 3, 12 * w + c + 6
                    if at < 6 and col < 24:
                        own[row, l * 144 + at * 24 + col] = 1
                    else:
                        recv[row, place[l, at % 6, col % 24]] = 1
    return send, own, recv


def step(index, by, count):
    return lax.rem(index + (by + count), count)


def block_kernel(nlat, nlon, norm, x_hbm, c_hbm, wq_hbm, wp_hbm, tab_hbm, idx_hbm, reg_hbm,
                 take_hbm, own_hbm, put_hbm, take_t_hbm, own_t_hbm, put_t_hbm,
                 xo_ref, co_ref, gq_ref, gp_ref, to_ref,
                 x_ref, c_ref, wq_ref, wp_ref, tab_ref, idx_ref, reg_ref,
                 take_ref, own_ref, put_ref, take_t_ref, own_t_ref, put_t_ref,
                 xw_s, cw_s, words_s, rows_of_table, idx_s, tail_s, bias_s, qkv_s, qkvt_s, gm_s, gmt_s, mixt_s, gqt_s, gp_s,
                 unit_s, inv_s, normt_s, gs_s, acc_s, branch_s, rows_s, g_s, tpart,
                 send_in, recv_in, send, recv, gsend, gcore, lat_send, lat_recv, turn, turned, ypart, ysend, yrecv,
                 zpart, zrecv, gs_send, gs_recv, tsend, trecv, tz, tfull,
                 load_sem, in_ss, in_rs, halo_ss, halo_rs, core_ss, core_rs, lat_ss, lat_rs,
                 y_ss, y_rs, z_ss, z_rs, t_ss, t_rs, tz_ss, tz_rs, tg_ss, tg_rs, gs_ss, gs_rs):
    nz = nlon // 8
    lev, lat, lon = lax.axis_index("lev"), lax.axis_index("lat"), lax.axis_index("lon")
    z, y = lon // 8, lax.rem(lon, 8)
    owner = lev * 8 + y

    def at_owner(o):
        return {"lev": o // 8, "lat": lat, "lon": z * 8 + lax.rem(o, 8)}

    core_peer = {"lev": 1 - lev, "lat": lat, "lon": lon}
    lat_peers = [{"lev": lev, "lat": step(lat, d, nlat), "lon": lon} for d in range(1, nlat)]
    y_peers = [{"lev": lev, "lat": lat, "lon": z * 8 + step(y, d, 8)} for d in range(1, 8)]
    z_peers = [{"lev": lev, "lat": lat, "lon": step(z, d, nz) * 8 + y} for d in range(1, nz)]
    owners = [at_owner(step(owner, d, 16)) for d in range(1, 16)]
    after, before = [
        [{"lev": lev, "lat": step(lat, by, nlat), "lon": lon},
         {"lev": lev, "lat": lat, "lon": step(lon, by, nlon)},
         {"lev": lev, "lat": step(lat, by, nlat), "lon": step(lon, by, nlon)}] for by in (1, -1)]
    barrier = pltpu.get_barrier_semaphore()
    greet = after[1:] + before[1:] + lat_peers + owners + z_peers
    for device in greet:
        pl.semaphore_signal(barrier, inc=1, device_id=device, device_id_type=MESH)

    names = ("x", "c", "take", "own", "put", "tab", "idx", "reg", "wq", "wp", "own_t", "take_t", "put_t")
    from_to = ((x_hbm, x_ref), (c_hbm, c_ref), (take_hbm, take_ref), (own_hbm, own_ref), (put_hbm, put_ref),
                (tab_hbm, tab_ref), (idx_hbm, idx_ref), (reg_hbm, reg_ref), (wq_hbm, wq_ref), (wp_hbm, wp_ref),
                (own_t_hbm, own_t_ref), (take_t_hbm, take_t_ref), (put_t_hbm, put_t_ref))
    loads = {}
    for n, (name, (src, dst)) in enumerate(zip(names, from_to)):
        loads[name] = pltpu.make_async_copy(src, dst, load_sem.at[n])
        loads[name].start()

    def push(src, dst, ss, rs, device):
        copy = pltpu.make_async_remote_copy(
            src_ref=src, dst_ref=dst, send_sem=ss, recv_sem=rs, device_id=device, device_id_type=MESH)
        copy.start()
        return copy

    for name in ("x", "c", "take"):
        loads[name].wait()
    for f, ref in enumerate((x_ref, c_ref)):
        send_in[f] = dot(take_ref[...], ref[...]).astype(BF16)
    pl.semaphore_wait(barrier, len(greet))
    arrive = [push(send_in.at[f, pl.ds(at, size)], recv_in.at[f, pl.ds(at, size)],
                   in_ss.at[3 * f + n], in_rs.at[3 * f + n], before[n])
              for f in range(2) for n, (at, size) in enumerate(PIECES)]

    for name in ("tab", "idx"):
        loads[name].wait()
    words_s[...] = jnp.zeros_like(words_s)
    for h in range(HEADS):
        rows_of_table[h:h + 1, :] = tab_ref[h]
    upper = jnp.floor(rows_of_table[0:6, :] * GRAIN + 0.5).astype(jnp.int32)
    lower = jnp.floor(rows_of_table[6:12, :] * GRAIN + 0.5).astype(jnp.int32)
    words_s[0:6, 0:POS] = jnp.left_shift(upper, 16) + jnp.bitwise_and(lower, 65535)
    index_t = idx_ref[...].T
    idx_s[0:WIN, :] = index_t[:, 0:128]
    idx_s[WIN:168, :] = pack_tail(index_t[:, 128:144])

    def look_up(r, store):
        at = pl.multiple_of(r * 8, 8)
        entry = idx_s[pl.ds(at, 8), :]
        low = jnp.bitwise_and(entry, 127)
        high = jnp.right_shift(entry, 7)
        found = [jnp.zeros((8, 128), jnp.int32) for _ in range(6)]
        for k in range(26):
            here = high == k
            for h in range(6):
                line = jnp.broadcast_to(words_s[h:h + 1, 128 * k:128 * k + 128], (8, 128))
                got = jnp.take_along_axis(line, low, axis=1, mode="promise_in_bounds")
                found[h] = jnp.where(here, got, found[h])
        for h in range(6):
            store(h, at, jnp.right_shift(found[h], 16).astype(F32) * (1 / GRAIN))
            half = jnp.right_shift(jnp.left_shift(found[h], 16), 16)
            store(h + 6, at, half.astype(F32) * (1 / GRAIN))

    def main_rows(r, carry):
        def store(h, at, value):
            bias_s[h, pl.ds(at, 8), 0:128] = value
        look_up(r, store)
        return carry

    def tail_rows(r, carry):
        def store(h, at, value):
            tail_s[h, pl.ds(pl.multiple_of(at - WIN, 8), 8), :] = value
        look_up(r, store)
        return carry

    lax.fori_loop(0, 18, main_rows, 0)
    lax.fori_loop(18, 21, tail_rows, 0)

    def spread(h, carry):
        for at in range(0, WIN, 8):
            q, b = at // 64, at % 64 // 8
            bias_s[h, at:at + 8, 128:144] = tail_s[h, 8 * q:8 * q + 8, 16 * b:16 * b + 16]
        return carry

    lax.fori_loop(0, HEADS, spread, 0)
    gs_s[...] = jnp.zeros_like(gs_s)

    loads["reg"].wait()
    region = reg_ref[...].astype(F32).astype(BF16)
    col_of = lax.broadcasted_iota(jnp.int32, (24, WIN), 0)
    place = lax.broadcasted_iota(jnp.int32, (24, WIN), 1)
    row_of = lax.broadcasted_iota(jnp.int32, (6, WIN), 0)
    row_at = lax.rem(lax.broadcasted_iota(jnp.int32, (6, WIN), 1), 72) // 12
    allowed = []
    for w in range(2):
        choose = jnp.where(col_of == lax.rem(place, 12) + 12 * w, 1.0, 0.0).astype(BF16)
        line = jnp.sum(jnp.where(row_of == row_at, dot(region, choose), 0.0), axis=0, keepdims=True)
        down = jnp.broadcast_to(line, (128, WIN)).T
        allowed.append(down[:, 0:1] == line)

    loads["own"].wait()
    loads["put"].wait()
    mine = [dot(own_ref[...], ref[...]) for ref in (x_ref, c_ref)]

    def assemble(f, ref):
        for copy in arrive[3 * f:3 * f + 3]:
            copy.wait()
        ref[...] = (mine[f] + dot(put_ref[...], recv_in[f])).astype(BF16)

    assemble(0, xw_s)

    loads["wq"].wait()
    loads["wp"].wait()
    flat = xw_s[...].astype(F32)
    center = flat - jnp.mean(flat, axis=-1, keepdims=True)
    inverse = lax.rsqrt(jnp.mean(center * center, axis=-1, keepdims=True) + 1e-05)
    unit = center * inverse
    unit_s[...] = unit
    inv_s[...] = jnp.broadcast_to(inverse, inv_s.shape)
    normed = unit.astype(BF16)
    packed = dot(normed, wq_ref[...]).astype(BF16)
    for w in range(2):
        at = slice(WIN * w, WIN * w + WIN)
        qkv_s[w] = packed[at]
        qkvt_s[w] = packed[at].T
        normt_s[w] = normed[at].T
    assemble(1, cw_s)
    cot = cw_s[...]
    gm_s[...] = dot_nt(cot, wp_ref[...]).astype(BF16)
    for w in range(2):
        at = slice(WIN * w, WIN * w + WIN)
        gmt_s[w] = dot_nt(wp_ref[...], cot[at]).astype(BF16)

    lane = lax.broadcasted_iota(jnp.int32, (WIN, 128), 1)
    line_of = lax.broadcasted_iota(jnp.int32, (128, WIN), 0)

    for g in range(3):
        off = 128 * g
        grad_key = [None, None]
        grad_value = [None, None]
        for a in range(4):
            h = g * 4 + a
            own_line = (line_of >= 32 * a) & (line_of < 32 * a + 32)
            own_lane = (lane >= 32 * a) & (lane < 32 * a + 32)
            total = None
            bias = bias_s[h]
            for w in range(2):
                q = qkv_s[w, :, pl.ds(off, 128)]
                k = qkv_s[w, :, pl.ds(off + 384, 128)]
                v = qkv_s[w, :, pl.ds(off + 768, 128)]
                qt = qkvt_s[w, pl.ds(off, 128), :]
                gmt = gmt_s[w, pl.ds(off, 128), :]
                here = off + 32 * a
                kt = qkvt_s[w, pl.ds(384 + here, 32), :]
                vt = qkvt_s[w, pl.ds(768 + here, 32), :]
                gm = gm_s[pl.ds(WIN * w, WIN), pl.ds(off, 128)]
                zero = jnp.zeros((), BF16)
                s = dot(k, jnp.where(own_line, qt, zero)) * FACTOR + bias
                s = jnp.where(allowed[w], s, -1e30)
                e = jnp.exp(s - jnp.max(s, axis=0, keepdims=True))
                p = e * (1.0 / jnp.sum(e, axis=0, keepdims=True))
                pb = p.astype(BF16)
                mixt_s[w, pl.ds(here, 32), :] = dot(vt, pb).astype(BF16)
                gpr = dot(v, jnp.where(own_line, gmt, zero))
                gv = dot(pb, gm)
                gs = p * (gpr - jnp.sum(p * gpr, axis=0, keepdims=True))
                sc = (gs * FACTOR).astype(BF16)
                gqt_s[w, pl.ds(here, 32), :] = dot(kt, sc).astype(BF16)
                gk = dot(sc, q)
                grad_key[w] = gk if a == 0 else jnp.where(own_lane, gk, grad_key[w])
                grad_value[w] = gv if a == 0 else jnp.where(own_lane, gv, grad_value[w])
                total = gs if w == 0 else total + gs
            at = slice(h % 6, h % 6 + 1)
            gs_s[h // 6, 0:WIN, at, :] = total[:, 0:128].reshape(WIN, 1, 128)
            gs_s[h // 6, WIN:168, at, :] = pack_tail(total[:, 128:144]).reshape(24, 1, 128)
        for w in range(2):
            rows = slice(WIN * w, WIN * w + WIN)
            gp_s[rows, pl.ds(off + 384, 128)] = grad_key[w].astype(BF16)
            gp_s[rows, pl.ds(off + 768, 128)] = grad_value[w].astype(BF16)

    gs_send[...] = gs_s[1 - lev].reshape(1344, 128).astype(BF16)
    swap = push(gs_send, gs_recv, gs_ss.at[0], gs_rs.at[0], core_peer)

    for w in range(2):
        gp_s[WIN * w:WIN * w + WIN, 0:384] = gqt_s[w].T
    for half in range(2):
        part = [dot(normt_s[w], gp_s[WIN * w:WIN * w + WIN, 576 * half:576 * half + 576]) for w in range(2)]
        g_s[half, :, 0:576] = part[0] + part[1]
        part = [dot(mixt_s[w], cw_s[WIN * w:WIN * w + WIN, 192 * half:192 * half + 192]) for w in range(2)]
        g_s[half, :, 576:768] = part[0] + part[1]
    gsend[...] = g_s[1 - lev].astype(BF16)
    lat_rows = [pl.ds(pl.multiple_of(48 * step(lat, d, nlat), 48), 48) for d in range(1, nlat + 1)]
    core = [push(gsend.at[rows], gcore.at[rows], core_ss.at[n], core_rs.at[n], core_peer)
            for n, rows in enumerate(lat_rows)]

    loads["put_t"].wait()
    for w in range(2):
        branch_s[WIN * w:WIN * w + WIN, :] = dot(mixt_s[w].T, wp_ref[...]).astype(BF16)
    send[0] = dot(put_t_ref[...], branch_s[...]).astype(BF16)

    over_lat = []
    for n in range(nlat - 1):
        core[n].wait()
        lat_send[n] = (g_s[lev, lat_rows[n], :] + gcore[lat_rows[n], :].astype(F32)).astype(BF16)
        over_lat.append(push(lat_send.at[n], lat_recv.at[n], lat_ss.at[n], lat_rs.at[n], lat_peers[n]))
    core[nlat - 1].wait()

    def halo_out(f):
        return [push(send.at[f, pl.ds(at, size)], recv.at[f, pl.ds(at, size)],
                     halo_ss.at[3 * f + n], halo_rs.at[3 * f + n], after[n])
                for n, (at, size) in enumerate(PIECES)]

    halo = halo_out(0)

    acc_s[...] = jnp.zeros_like(acc_s)
    low_of = lax.broadcasted_iota(jnp.int32, (256, 128), 0)

    def pairs(r, carry):
        entry = idx_s[pl.ds(pl.multiple_of(r * 8, 8), 8), :]
        low = jnp.bitwise_and(entry, 255)
        high = jnp.right_shift(entry, 8)
        other = gs_recv[pl.ds(pl.multiple_of(r * 64, 64), 64), :].astype(F32)
        both = gs_s[lev, pl.ds(r * 8, 8)] + other.reshape(8, 8, 128)
        lefts = []
        rights = []
        for s in range(8):
            value = both[s]
            lefts.append(jnp.concatenate(
                [jnp.where(high[s:s + 1, :] == k, value, 0.0) for k in range(13)], 0).astype(BF16))
            rights.append(jnp.where(low[s:s + 1, :] == low_of, 1.0, 0.0).astype(BF16))
        acc_s[...] += dot_nt(jnp.concatenate(lefts, 1), jnp.concatenate(rights, 1))
        return carry

    swap.wait()
    lax.fori_loop(0, 21, pairs, 0, unroll=3)
    tpart[...] = jnp.zeros_like(tpart)
    for k in range(13):
        tpart[16 * k:16 * k + 8, :] = acc_s[8 * k:8 * k + 8, 0:128]
        tpart[16 * k + 8:16 * k + 16, :] = acc_s[8 * k:8 * k + 8, 128:256]
    tsend[...] = tpart[...].astype(BF16)
    table = [push(tsend.at[pl.ds(pl.multiple_of(32 * step(y, d, 8), 32), 32)],
                  trecv.at[d - 1], t_ss.at[d - 1], t_rs.at[d - 1], y_peers[d - 1])
             for d in range(1, 8)]

    gn = dot_nt(gp_s[...], wq_ref[...])
    unit = unit_s[...]
    rows_s[...] = (inv_s[:, 0:1] * (
        gn - jnp.mean(gn, axis=-1, keepdims=True)
        - unit * jnp.mean(gn * unit, axis=-1, keepdims=True))).astype(BF16)
    send[1] = dot(put_t_ref[...], rows_s[...]).astype(BF16)

    halo += halo_out(1)

    part = tpart[pl.ds(pl.multiple_of(32 * y, 32), 32), :]
    for n in range(7):
        table[n].wait()
        part = part + trecv[n].astype(F32)
    tz[z] = part
    over_z = [push(tz.at[z], tz.at[z], tz_ss.at[n], tz_rs.at[n], z_peers[n]) for n in range(nz - 1)]

    total = g_s[lev, lat_rows[-1], :] + gcore[lat_rows[-1], :].astype(F32)
    for n in range(nlat - 1):
        over_lat[n].wait()
        total = total + lat_recv[n].astype(F32)
    turn[...] = jnp.zeros_like(turn)
    turn[0:48, :] = total
    turn[64:112, :] = total
    turned[...] = turn[...].T
    first = lax.broadcasted_iota(jnp.int32, (24, 128), 1) < 64
    for to in range(8):
        for p in range(nz // 2):
            a, b = 16 * p + to, 16 * p + 8 + to
            ypart[to, 24 * p:24 * p + 18, :] = jnp.where(
                first[0:18], turned[18 * a:18 * a + 18, :], turned[18 * b:18 * b + 18, :])
            ypart[to, 24 * p + 18:24 * p + 24, :] = jnp.where(
                first[0:6], turned[576 + 6 * a:576 + 6 * a + 6, :], turned[576 + 6 * b:576 + 6 * b + 6, :])
    ysend[...] = ypart[...].astype(BF16)
    over_y = [push(ysend.at[step(y, d, 8)], yrecv.at[d - 1], y_ss.at[d - 1], y_rs.at[d - 1], y_peers[d - 1])
              for d in range(1, 8)]

    for copy in over_z:
        copy.wait()
    part = tz[0]
    for n in range(1, nz):
        part = part + tz[n]
    own_block = pl.ds(pl.multiple_of(32 * owner, 32), 32)
    tfull[own_block, :] = part.astype(BF16)
    gathered = [push(tfull.at[own_block], tfull.at[own_block], tg_ss.at[n], tg_rs.at[n], owners[n])
                for n in range(15)]

    total = ypart[y]
    for n in range(7):
        over_y[n].wait()
        total = total + yrecv[n].astype(F32)
    zpart[...] = total
    last = [push(zpart.at[pl.ds(pl.multiple_of(24 * (step(z, d, nz) // 2), 24), 24)],
                 zrecv.at[d - 1], z_ss.at[d - 1], z_rs.at[d - 1], z_peers[d - 1])
            for d in range(1, nz)]

    loads["own_t"].wait()
    loads["take_t"].wait()
    for f, (base, ref, out) in enumerate(((x_ref, branch_s, xo_ref), (c_ref, rows_s, co_ref))):
        for copy in halo[3 * f:3 * f + 3]:
            copy.wait()
        rolled = dot(own_t_ref[...], ref[...]) + dot(take_t_ref[...], recv[f])
        out[...] = (base[...].astype(F32) + rolled).astype(BF16)

    total = zpart[pl.ds(pl.multiple_of(24 * (z // 2), 24), 24), :]
    for n in range(nz - 1):
        last[n].wait()
        total = total + zrecv[n]
    total = jnp.where(lax.rem(z, 2) == 0, total[:, 0:48], total[:, 64:112]) * norm
    gq_ref[...] = total[0:18]
    gp_ref[...] = total[18:24]

    for n in range(15):
        gathered[n].wait()
    full = tfull[...].astype(F32)
    for k in range(26):
        width = min(128, POS - 128 * k)
        for h in range(HEADS):
            at = 256 * (h // 6) + 8 * k + h % 6
            to_ref[h, :, 128 * k:128 * k + width] = full[at:at + 1, 0:width]


def block(nlat, nlon, norm, *operands):
    nz = nlon // 8
    sem = pltpu.SemaphoreType.DMA
    vmem = pltpu.VMEM
    loaded = [operands[n] for n in range(13)]
    return pl.pallas_call(
        functools.partial(block_kernel, nlat, nlon, norm),
        in_specs=[pl.BlockSpec(memory_space=pl.ANY)] * 13,
        out_shape=[
            jax.ShapeDtypeStruct((288, 384), BF16),
            jax.ShapeDtypeStruct((288, 384), BF16),
            jax.ShapeDtypeStruct((18, 48), F32),
            jax.ShapeDtypeStruct((6, 48), F32),
            jax.ShapeDtypeStruct((HEADS, 1, POS), F32),
        ],
        scratch_shapes=[vmem(a.shape, a.dtype) for a in loaded] + [
            vmem((288, 384), BF16),
            vmem((288, 384), BF16),
            vmem((8, 3328), jnp.int32),
            vmem((16, POS), F32),
            vmem((168, 128), jnp.int32),
            vmem((12, 24, 128), F32),
            vmem((12, 144, 144), F32),
            vmem((2, 144, 1152), BF16),
            vmem((2, 1152, 144), BF16),
            vmem((288, 384), BF16),
            vmem((2, 384, 144), BF16),
            vmem((2, 384, 144), BF16),
            vmem((2, 384, 144), BF16),
            vmem((288, 1152), BF16),
            vmem((288, 384), F32),
            vmem((288, 128), F32),
            vmem((2, 384, 144), BF16),
            vmem((2, 168, 8, 128), F32),
            vmem((104, 256), F32),
            vmem((288, 384), BF16),
            vmem((288, 384), BF16),
            vmem((2, 384, 768), F32),
            vmem((256, 128), F32),
            vmem((2, 208, 384), BF16),
            vmem((2, 208, 384), BF16),
            vmem((2, 208, 384), BF16),
            vmem((2, 208, 384), BF16),
            vmem((384, 768), BF16),
            vmem((384, 768), BF16),
            vmem((nlat - 1, 48, 768), BF16),
            vmem((nlat - 1, 48, 768), BF16),
            vmem((128, 768), F32),
            vmem((768, 128), F32),
            vmem((8, 48, 128), F32),
            vmem((8, 48, 128), BF16),
            vmem((7, 48, 128), BF16),
            vmem((48, 128), F32),
            vmem((nz - 1, 24, 128), F32),
            vmem((1344, 128), BF16),
            vmem((1344, 128), BF16),
            vmem((256, 128), BF16),
            vmem((7, 32, 128), BF16),
            vmem((nz, 32, 128), F32),
            vmem((512, 128), BF16),
            sem((13,)), sem((6,)), sem((6,)), sem((6,)), sem((6,)), sem((nlat,)), sem((nlat,)),
            sem((nlat - 1,)), sem((nlat - 1,)),
            sem((7,)), sem((7,)), sem((nz - 1,)), sem((nz - 1,)),
            sem((7,)), sem((7,)), sem((nz - 1,)), sem((nz - 1,)), sem((15,)), sem((15,)), sem((1,)), sem((1,)),
        ],
        compiler_params=pltpu.CompilerParams(
            collective_id=0, has_side_effects=True, vmem_limit_bytes=56 * 1024 * 1024),
        name="block",
    )(*operands)


def publish_kernel(*refs):
    results, outs, held = refs[0:5], refs[5:10], refs[10:15]
    in_sem, out_sem = refs[15:]
    loads = [pltpu.make_async_copy(results[n], held[n], in_sem.at[n]) for n in range(5)]
    stores = [pltpu.make_async_copy(held[n], outs[n], out_sem.at[n]) for n in range(5)]
    for copy in loads:
        copy.start()
    for n in range(5):
        loads[n].wait()
        stores[n].start()
    for copy in stores:
        copy.wait()


def publish(*results):
    sem = pltpu.SemaphoreType.DMA
    return pl.pallas_call(
        publish_kernel,
        in_specs=[pl.BlockSpec(memory_space=pl.ANY)] * 5,
        out_specs=[pl.BlockSpec(memory_space=pl.ANY)] * 5,
        out_shape=[jax.ShapeDtypeStruct(r.shape, r.dtype) for r in results],
        scratch_shapes=[pltpu.VMEM(r.shape, r.dtype) for r in results] + [sem((5,)), sem((5,))],
        compiler_params=pltpu.CompilerParams(vmem_limit_bytes=56 * 1024 * 1024),
        name="publish",
    )(*results)


def body(tokens, cotangent, w_qkv, w_proj, bias_table, bias_index, region_ids):
    levels, rows, columns, width = tokens.shape
    nlev, nlat, nlon = lax.axis_size("lev"), lax.axis_size("lat"), lax.axis_size("lon")
    norm = 1.0 / math.sqrt(levels * nlev * rows * nlat * columns * nlon)
    send, own, recv = permutations()
    send, own, recv, send_t, own_t, recv_t = [
        jnp.asarray(m, BF16) for m in (send, own, recv, send.T, own.T, recv.T)]
    results = block(
        nlat, nlon, norm, tokens.reshape(288, width), cotangent.reshape(288, width), w_qkv, w_proj,
        bias_table.transpose(1, 0, 2), bias_index[0], region_ids, send, own, recv, send_t, own_t, recv_t)
    block_out, grad_tokens, gq, gp, table = publish(*results)
    return (block_out.reshape(tokens.shape), grad_tokens.reshape(tokens.shape), gq.T, gp.T,
            table.transpose(1, 0, 2))


def solution(mesh):
    return jax.shard_map(
        body,
        mesh=mesh,
        in_specs=(
            jax.P("lev", "lat", "lon", None),
            jax.P("lev", "lat", "lon", None),
            jax.P(),
            jax.P(),
            jax.P("lat", None, None),
            jax.P("lat", None, None),
            jax.P("lat", "lon"),
        ),
        out_specs=(
            jax.P("lev", "lat", "lon", None),
            jax.P("lev", "lat", "lon", None),
            jax.P("lat", ("lev", "lon")),
            jax.P("lat", ("lev", "lon")),
            jax.P("lat", None, None),
        ),
        check_vma=False,
    )
```
